256 devices in a mesh: seq: 64 (over z, y, core), tensor: 4 (over x).
Axes of the slice: x: 4, y: 4, z: 8, core: 2. Of those that a mesh axis runs over, the one named last changes fastest.
Arguments:
- byte_rows: bfloat16 [32768, 1024], P('seq'), may hold values from -6 to 6
- patch_lengths: int32 [64, 128], P('seq'), may hold values from 1 to 16, 512 in all within a row
- pool_query: bfloat16 [1024, 1024], P(None, 'tensor')
- pool_key: bfloat16 [1024, 1024], P(None, 'tensor')
- pool_value: bfloat16 [1024, 1024], P(None, 'tensor'), may hold values from -0.1875 to 0.1875
- pool_out: bfloat16 [1024, 4096], P('tensor'), may hold values from -0.1875 to 0.1875
- norm_gain: bfloat16 [4096], replicated, may hold values from 0.5 to 1.5
- query_weight: bfloat16 [4096, 2048], P('seq', 'tensor')
- key_weight: bfloat16 [4096, 512], P(None, 'tensor')
- value_weight: bfloat16 [4096, 512], P(None, 'tensor'), may hold values from -0.09375 to 0.09375
- out_weight: bfloat16 [2048, 4096], P('tensor'), may hold values from -0.125 to 0.125
- cotangent: bfloat16 [8192, 4096], P(('seq', 'tensor')), may hold values from -6 to 6
Outputs:
- layer_out: bfloat16 [8192, 4096], P(('seq', 'tensor'))
- patch_grad: bfloat16 [8192, 4096], P(('seq', 'tensor'))
The draws below stay inside these ranges and needn't reach their ends.
Inputs may be any that keep to these rules, and one draw needn't show every extreme that they name: `patch_lengths`: every patch holds at least one byte.
All inputs are finite; a program needn't handle non-finite values.
Results may differ from the reference program's by a relative error of at most 0.03.
Values may be sent and summed in bfloat16 or wider, within the bound.
A program may use at most 128 MiB of HBM per device.

```python
import math
import jax
import jax.numpy as jnp
import numpy as np
from jax import lax

D = 4096
DB = 1024
HDIM = 128
PH = 8
QH = 16
KVH = 4
LMAX = 16
P_SEQ = 128
B_DEV = 512
NP = 8192
NB = 32768
N_SEQ = 64


def query_like(key, salt, rows, heads, spread):
    key = jax.random.fold_in(key, salt + 1000)
    noise = jax.random.normal(key, (rows, heads * HDIM), jnp.float32) * rows ** (-0.5)
    weights = noise * spread
    return weights.astype(jnp.bfloat16)


def key_like(key, salt, rows, kv_heads):
    key = jax.random.fold_in(key, salt + 2000)
    noise = jax.random.normal(key, (rows, kv_heads * HDIM), jnp.float32) * rows ** (-0.5)
    weights = noise
    return weights.astype(jnp.bfloat16)


def draw_pool_query(key, part):
    return query_like(key, 7, DB, PH, 1.0)


def draw_pool_key(key, part):
    return key_like(key, 7, DB, PH)


def draw_query_weight(key, part):
    return query_like(key, 3, D, QH, 3.0)


def draw_key_weight(key, part):
    return key_like(key, 3, D, KVH)


def block_scale(stream_key, dims, cuts, least, high):
    level, own = 1.0, jax.random.fold_in(stream_key, 6)
    for dim, blocks in cuts:
        draws = jnp.exp(jax.random.uniform(jax.random.fold_in(own, dim), (blocks,), jnp.float32, least / len(cuts), high / len(cuts)))
        level = level * jnp.repeat(draws, dims[dim] // blocks).reshape([-1 if axis == dim else 1 for axis in range(len(dims))])
    return level


def profile(number_of, total, limit, skew):
    weights = [(1 << 20) // math.isqrt(rank ** skew) + 1 for rank in range(2, number_of + 1)]
    rest, counts = total - limit - (number_of - 1), [1] * (number_of - 1)
    while rest > 0:
        candidates = [i for i in range(number_of - 1) if counts[i] < limit]
        pool, left = sum([weights[i] for i in candidates]), rest
        for i in candidates:
            extra = min(limit - counts[i], max(1, left * weights[i] // pool), rest)
            counts[i] = counts[i] + extra
            rest = rest - extra
    return np.array([limit] + counts)


def uneven(own_key, amount, total, reach, skew):
    if amount == 2:
        one = jax.random.randint(own_key, (), max(1, total - reach), min(reach, total - 1) + 1)
        return jnp.stack([one, total - one])
    tallies = jnp.asarray(profile(amount, total, reach, skew), jnp.int32)
    pairs = (amount - 1) // 2
    giver, taker = tallies[1:1 + 2 * pairs:2], tallies[2:2 + 2 * pairs:2]
    margin = jnp.minimum(giver - 1, reach - taker)
    passed = jax.random.randint(jax.random.fold_in(own_key, 1), (pairs,), 0, 1 << 20) % (margin + 1)
    tallies = tallies.at[1:1 + 2 * pairs:2].set(giver - passed).at[2:2 + 2 * pairs:2].set(taker + passed)
    return tallies[jax.random.permutation(jax.random.fold_in(own_key, 2), amount)]


def normal_values(key, extent, width, most, pieces=(), kind=jnp.bfloat16):
    gain = block_scale(key, extent, pieces, -0.22, 0.18) if pieces else 1.0
    entries = jax.random.normal(key, extent, jnp.float32) * width * gain
    return jnp.minimum(jnp.maximum(entries, -most), most).astype(kind)


def setup_inputs(seed: int = 0) -> dict:
    seeds = jax.random.split(jax.random.key(seed), 13)
    byte_rows = normal_values(seeds[0], (NB, DB), 1.0, 6.0, ((0, 64),))
    patch_lengths = jax.vmap(lambda own: uneven(own, P_SEQ, B_DEV, LMAX, 2))(jax.random.split(seeds[1], N_SEQ)).reshape((N_SEQ, P_SEQ)).astype(jnp.int32)
    pool_query = draw_pool_query(jax.random.fold_in(seeds[12], 71), 0)
    pool_key = draw_pool_key(jax.random.fold_in(seeds[12], 71), 0)
    pool_value = normal_values(seeds[4], (DB, DB), DB ** -0.5, 0.1875, ((1, 4),))
    pool_out = normal_values(seeds[5], (DB, D), DB ** -0.5, 0.1875, ((0, 4),))
    norm_gain = jnp.clip(1.0 + 0.1 * jax.random.normal(seeds[6], (D,), jnp.float32), 0.5, 1.5).astype(jnp.bfloat16)
    query_weight = draw_query_weight(jax.random.fold_in(seeds[12], 71), 0)
    key_weight = draw_key_weight(jax.random.fold_in(seeds[12], 71), 0)
    value_weight = normal_values(seeds[9], (D, KVH * HDIM), D ** -0.5, 0.09375, ((1, 4),))
    out_weight = normal_values(seeds[10], (QH * HDIM, D), (QH * HDIM) ** -0.5, 0.125, ((0, 4),))
    cotangent = normal_values(seeds[11], (NP, D), 1.0, 6.0, ((0, 256),))
    return {"byte_rows": byte_rows, "patch_lengths": patch_lengths, "pool_query": pool_query, "pool_key": pool_key, "pool_value": pool_value, "pool_out": pool_out, "norm_gain": norm_gain, "query_weight": query_weight, "key_weight": key_weight, "value_weight": value_weight, "out_weight": out_weight, "cotangent": cotangent}


EPS = 1e-05
NEG = -1e+30

def pool_shard(byte_block, lengths, pool_query, pool_key, pool_value, pool_out):
    ends = jnp.cumsum(lengths)
    starts = ends - lengths
    where_at = jnp.arange(byte_block.shape[0], dtype=jnp.int32)
    member = (where_at[None, :] >= starts[:, None]) & (where_at[None, :] < ends[:, None])
    sums = jnp.dot(member.astype(jnp.bfloat16), byte_block, preferred_element_type=jnp.float32)
    means = (sums / lengths[:, None].astype(jnp.float32)).astype(jnp.bfloat16)
    pool_q = jnp.dot(means, pool_query, preferred_element_type=jnp.float32).astype(jnp.bfloat16)
    pool_k = jnp.dot(byte_block, pool_key, preferred_element_type=jnp.float32).astype(jnp.bfloat16)
    pool_v = jnp.dot(byte_block, pool_value, preferred_element_type=jnp.float32).astype(jnp.bfloat16)
    heads = pool_query.shape[1] // HDIM
    q_heads = pool_q.reshape(-1, heads, HDIM).astype(jnp.float32)
    k_heads = pool_k.reshape(-1, heads, HDIM).astype(jnp.float32)
    v_heads = pool_v.reshape(-1, heads, HDIM).astype(jnp.float32)
    scores = jnp.einsum('phd,bhd->hpb', q_heads, k_heads) * HDIM ** (-0.5)
    scores = jnp.where(member[None], scores, NEG)
    top = lax.optimization_barrier(jnp.max(scores, -1, keepdims=True))
    expo = jnp.exp(scores - top)
    weights = (expo / lax.optimization_barrier(jnp.sum(expo, -1, keepdims=True))).astype(jnp.bfloat16)
    pooled = jnp.einsum('hpb,bhd->phd', weights.astype(jnp.float32), v_heads)
    pooled = pooled.reshape(lengths.shape[0], -1).astype(jnp.bfloat16)
    return jnp.dot(pooled, pool_out, preferred_element_type=jnp.float32)

def reference(byte_rows, patch_lengths, pool_query, pool_key, pool_value, pool_out, norm_gain, query_weight, key_weight, value_weight, out_weight, cotangent):
    shards = byte_rows.reshape(N_SEQ, B_DEV, DB)

    def pool_one(item):
        return pool_shard(item[0], item[1], pool_query, pool_key, pool_value, pool_out).astype(jnp.bfloat16)
    patches = lax.map(pool_one, (shards, patch_lengths)).reshape(NP, D)
    hidden = patches.astype(jnp.float32)
    inv = lax.rsqrt(lax.optimization_barrier(jnp.mean(hidden * hidden, -1, keepdims=True)) + EPS)
    unit = hidden * inv
    normed = (unit * norm_gain.astype(jnp.float32)).astype(jnp.bfloat16)
    queries = jnp.dot(normed, query_weight, preferred_element_type=jnp.float32).astype(jnp.bfloat16)
    keys = jnp.dot(normed, key_weight, preferred_element_type=jnp.float32).astype(jnp.bfloat16)
    values = jnp.dot(normed, value_weight, preferred_element_type=jnp.float32).astype(jnp.bfloat16)
    group = QH // KVH
    scale = HDIM ** (-0.5)
    k_heads = keys.reshape(NP, KVH, HDIM).astype(jnp.float32)
    v_heads = values.reshape(NP, KVH, HDIM).astype(jnp.float32)
    key_pos = jnp.arange(NP, dtype=jnp.int32)
    q_blocks = queries.reshape(N_SEQ, P_SEQ, KVH, group, HDIM)
    firsts = (jnp.arange(N_SEQ, dtype=jnp.int32) * P_SEQ).astype(jnp.int32)

    def masked_scores(q_block, first):
        q_pos = first + jnp.arange(P_SEQ, dtype=jnp.int32)
        scores = jnp.einsum('qjgd,kjd->jgqk', q_block.astype(jnp.float32), k_heads) * scale
        return jnp.where(key_pos[None, :] <= q_pos[:, None], scores, NEG)

    def attend(item):
        q_block, first = item
        scores = masked_scores(q_block, first)
        top = lax.optimization_barrier(jnp.max(scores, -1, keepdims=True))
        lse = top + jnp.log(lax.optimization_barrier(jnp.sum(jnp.exp(scores - top), -1, keepdims=True)))
        weights = jnp.exp(scores - lse).astype(jnp.bfloat16)
        out = jnp.einsum('jgqk,kjd->qjgd', weights.astype(jnp.float32), v_heads)
        return (out.reshape(P_SEQ, QH * HDIM).astype(jnp.bfloat16), lse[..., 0])
    attn_blocks, lses = lax.map(attend, (q_blocks, firsts))
    attn = attn_blocks.reshape(NP, QH * HDIM)
    layer_out = (hidden + jnp.dot(attn, out_weight, preferred_element_type=jnp.float32)).astype(jnp.bfloat16)
    grad_attn = jnp.dot(cotangent, out_weight.T, preferred_element_type=jnp.float32).astype(jnp.bfloat16)
    g_blocks = grad_attn.reshape(N_SEQ, P_SEQ, KVH, group, HDIM)
    o_blocks = attn.reshape(N_SEQ, P_SEQ, KVH, group, HDIM)

    def back(carry, item):
        q_block, o_block, g_block, lse, first = item
        scores = masked_scores(q_block, first)
        prob = jnp.exp(scores - lse[..., None])
        weights = prob.astype(jnp.bfloat16)
        g_float = g_block.astype(jnp.float32)
        dprob = jnp.einsum('qjgd,kjd->jgqk', g_float, v_heads)
        delta = jnp.einsum('qjgd,qjgd->jgq', g_float, o_block.astype(jnp.float32))
        dscore = (prob * (dprob - delta[..., None])).astype(jnp.bfloat16).astype(jnp.float32)
        grad_q = (jnp.einsum('jgqk,kjd->qjgd', dscore, k_heads) * scale).reshape(P_SEQ, QH * HDIM)
        grad_k = carry[0] + jnp.einsum('jgqk,qjgd->kjd', dscore, q_block.astype(jnp.float32)) * scale
        grad_v = carry[1] + jnp.einsum('jgqk,qjgd->kjd', weights.astype(jnp.float32), g_float)
        return ((grad_k, grad_v), grad_q.astype(jnp.bfloat16))
    zeros = jnp.zeros((NP, KVH, HDIM), jnp.float32)
    (grad_k, grad_v), grad_q = lax.scan(back, (zeros, zeros), (q_blocks, o_blocks, g_blocks, lses, firsts))
    grad_q = grad_q.reshape(NP, QH * HDIM)
    grad_k = grad_k.reshape(NP, KVH * HDIM).astype(jnp.bfloat16)
    grad_v = grad_v.reshape(NP, KVH * HDIM).astype(jnp.bfloat16)
    grad_normed = jnp.dot(grad_q, query_weight.T, preferred_element_type=jnp.float32)
    grad_normed = grad_normed + jnp.dot(grad_k, key_weight.T, preferred_element_type=jnp.float32)
    grad_normed = grad_normed + jnp.dot(grad_v, value_weight.T, preferred_element_type=jnp.float32)
    scaled = grad_normed * norm_gain.astype(jnp.float32)
    patch_grad = cotangent.astype(jnp.float32) + inv * (scaled - unit * lax.optimization_barrier(jnp.mean(scaled * unit, -1, keepdims=True)))
    return (layer_out, patch_grad.astype(jnp.bfloat16))
```

```python
import math

import jax
import jax.numpy as jnp
from jax import lax
from jax.experimental import pallas as pl
from jax.experimental.pallas import tpu as pltpu
from jax.sharding import PartitionSpec as P

EPS = 1e-05
NEG = -1e30
MESH = pl.DeviceIdType.MESH
NZ, NY, NX = 8, 4, 4
HD = 128
GROUP = 4
ROWS = 128
HALF = 64
SHARDS = 64
D = 4096
OWN = 32
KB = 512
VMEM = 56 * 1024 * 1024
F32 = jnp.float32
BF16 = jnp.bfloat16
NT = (((1,), (1,)), ((), ()))
TN = (((0,), (0,)), ((), ()))


def mm(a, b):
    return jnp.dot(a, b, preferred_element_type=F32)


def dg(a, b, dims):
    return lax.dot_general(a, b, dims, preferred_element_type=F32)


class Place:
    def __init__(self):
        s = lax.axis_index("seq")
        self.s = s
        self.z = lax.div(s, 8)
        self.y = lax.rem(lax.div(s, 2), 4)
        self.c = lax.rem(s, 2)
        self.t = lax.axis_index("tensor")
        self.sib = self.seq(self.z, self.y, 1 - self.c)
        self.up = self.seq(self.zz(1), self.y, self.c)
        self.down = self.seq(self.zz(-1), self.y, self.c)
        self.north = self.seq(self.z, self.yy(1), self.c)
        self.south = self.seq(self.z, self.yy(-1), self.c)
        self.twin = SHARDS - 1 - s

    def zz(self, i):
        return lax.rem(self.z + NZ + i, NZ)

    def yy(self, i):
        return lax.rem(self.y + NY + i, NY)

    def tt(self, i):
        return lax.rem(self.t + NX + i, NX)

    def seq(self, z, y, c):
        return (z * NY + y) * 2 + c


class Net:
    def __init__(self, send, recv):
        self.send, self.recv, self.all = send, recv, []

    def put(self, src, dst, **device):
        n = len(self.all)
        copy = pltpu.make_async_remote_copy(
            src_ref=src,
            dst_ref=dst,
            send_sem=self.send.at[n],
            recv_sem=self.recv.at[n],
            device_id=device,
            device_id_type=MESH,
        )
        copy.start()
        self.all.append(copy)
        return copy

    def finish(self):
        for copy in self.all:
            copy.wait_send()


def greet(devices):
    barrier = pltpu.get_barrier_semaphore()
    for device in devices:
        pl.semaphore_signal(barrier, inc=1, device_id=device, device_id_type=MESH)
    pl.semaphore_wait(barrier, len(devices))


def ring_partners(at):
    return [{"seq": d} for d in (at.sib, at.up, at.down, at.north, at.south)]


def line_partners(at):
    return [{"tensor": at.tt(1)}, {"tensor": at.tt(-1)}]


def run(chains):
    chains = list(chains)
    while chains:
        left = []
        for chain in chains:
            try:
                next(chain)
                left.append(chain)
            except StopIteration:
                pass
        chains = left


def same(net, view, **device):
    return net.put(view, view, **device)


def gather_zy(net, at, buf):
    rows = buf.shape[4] // 2
    zz, yy, c, y = at.zz, at.yy, at.c, at.y
    for i in range(1, 4):
        p = same(net, buf.at[zz(1 - i), y, c, 0], seq=at.up)
        m = same(net, buf.at[zz(i - 1), y, c, 0], seq=at.down)
        yield
        p.wait_recv()
        m.wait_recv()
    p = same(net, buf.at[zz(-3), y, c, 0, pl.ds(0, rows)], seq=at.up)
    m = same(net, buf.at[zz(3), y, c, 0, pl.ds(rows, rows)], seq=at.down)
    yield
    p.wait_recv()
    m.wait_recv()
    every = pl.ds(0, NZ)
    p = same(net, buf.at[every, y, c, 0], seq=at.north)
    m = same(net, buf.at[every, y, c, 0], seq=at.south)
    sib = [same(net, buf.at[every, y, c, 0], seq=at.sib)]
    yield
    p.wait_recv()
    m.wait_recv()
    p = same(net, buf.at[pl.ds(0, 4), yy(-1), c, 0], seq=at.north)
    m = same(net, buf.at[pl.ds(4, 4), yy(1), c, 0], seq=at.south)
    sib.append(same(net, buf.at[every, yy(-1), c, 0], seq=at.sib))
    sib.append(same(net, buf.at[every, yy(1), c, 0], seq=at.sib))
    yield
    p.wait_recv()
    m.wait_recv()
    sib.append(same(net, buf.at[every, yy(2), c, 0], seq=at.sib))
    yield
    for copy in sib:
        copy.wait_recv()


def gather_yz(net, at, buf):
    rows = buf.shape[4] // 2
    zz, yy, c, z = at.zz, at.yy, at.c, at.z
    p = same(net, buf.at[z, at.y, c, 1], seq=at.north)
    m = same(net, buf.at[z, at.y, c, 1], seq=at.south)
    yield
    p.wait_recv()
    m.wait_recv()
    p = same(net, buf.at[z, yy(-1), c, 1, pl.ds(0, rows)], seq=at.north)
    m = same(net, buf.at[z, yy(1), c, 1, pl.ds(rows, rows)], seq=at.south)
    yield
    p.wait_recv()
    m.wait_recv()
    every = pl.ds(0, NY)
    sib = [same(net, buf.at[z, every, c, 1], seq=at.sib)]
    for i in range(1, 4):
        p = same(net, buf.at[zz(1 - i), every, c, 1], seq=at.up)
        m = same(net, buf.at[zz(i - 1), every, c, 1], seq=at.down)
        yield
        p.wait_recv()
        m.wait_recv()
        sib.append(same(net, buf.at[zz(-i), every, c, 1], seq=at.sib))
        sib.append(same(net, buf.at[zz(i), every, c, 1], seq=at.sib))
    p = same(net, buf.at[zz(-3), pl.ds(0, 2), c, 1], seq=at.up)
    m = same(net, buf.at[zz(3), pl.ds(2, 2), c, 1], seq=at.down)
    yield
    p.wait_recv()
    m.wait_recv()
    sib.append(same(net, buf.at[zz(4), every, c, 1], seq=at.sib))
    yield
    for copy in sib:
        copy.wait_recv()


def gather_x(net, at, buf):
    rows = buf.shape[1] // 2
    tt = at.tt
    p = same(net, buf.at[at.t], tensor=tt(1))
    m = same(net, buf.at[at.t], tensor=tt(-1))
    yield
    p.wait_recv()
    m.wait_recv()
    p = same(net, buf.at[tt(-1), pl.ds(0, rows)], tensor=tt(1))
    m = same(net, buf.at[tt(1), pl.ds(rows, rows)], tensor=tt(-1))
    yield
    p.wait_recv()
    m.wait_recv()


def add_into(ref, other):
    ref[...] = (ref[...].astype(F32) + other[...].astype(F32)).astype(BF16)


def scatter_x(net, at, part, first, second, result):
    rows = part.shape[1] // 2
    tt = at.tt
    low, high = pl.ds(0, rows), pl.ds(rows, rows)
    p = net.put(part.at[tt(2), low], first.at[0], tensor=tt(1))
    m = net.put(part.at[tt(2), high], first.at[1], tensor=tt(-1))
    yield
    p.wait_recv()
    m.wait_recv()
    add_into(part.at[tt(1), low], first.at[0])
    add_into(part.at[tt(-1), high], first.at[1])
    p = net.put(part.at[tt(1)], second.at[0], tensor=tt(1))
    m = net.put(part.at[tt(-1)], second.at[1], tensor=tt(-1))
    yield
    p.wait_recv()
    m.wait_recv()
    result(part[at.t].astype(F32) + second[0].astype(F32) + second[1].astype(F32))


def scatter_yz(net, at, acc, y_first, y_second, z_first, z_next, out):
    yy, zz = at.yy, at.zz
    low, high = pl.ds(0, 4), pl.ds(4, 4)
    p = net.put(acc.at[yy(2), low], y_first.at[0], seq=at.north)
    m = net.put(acc.at[yy(2), high], y_first.at[1], seq=at.south)
    yield
    p.wait_recv()
    m.wait_recv()
    add_into(acc.at[yy(1), low], y_first.at[0])
    p = net.put(acc.at[yy(1)], y_second.at[0], seq=at.north)
    add_into(acc.at[yy(-1), high], y_first.at[1])
    m = net.put(acc.at[yy(-1)], y_second.at[1], seq=at.south)
    yield
    p.wait_recv()
    m.wait_recv()
    add_into(acc.at[at.y], y_second.at[0])
    add_into(acc.at[at.y], y_second.at[1])
    yield from scatter_line(net, acc.at[at.y], zz, at.up, at.down, z_first, z_next, out, ROWS // 2)


def scatter_zy(net, at, acc, z_first, z_next, y_first, y_second, out):
    yy = at.yy
    mine = acc.at[at.z]
    yield from scatter_line(net, acc, at.zz, at.up, at.down, z_first, z_next, None, NY // 2)
    low, high = pl.ds(0, ROWS // 2), pl.ds(ROWS // 2, ROWS // 2)
    p = net.put(mine.at[yy(2), low], y_first.at[0], seq=at.north)
    m = net.put(mine.at[yy(2), high], y_first.at[1], seq=at.south)
    yield
    p.wait_recv()
    m.wait_recv()
    add_into(mine.at[yy(1), low], y_first.at[0])
    add_into(mine.at[yy(-1), high], y_first.at[1])
    p = net.put(mine.at[yy(1)], y_second.at[0], seq=at.north)
    m = net.put(mine.at[yy(-1)], y_second.at[1], seq=at.south)
    yield
    p.wait_recv()
    m.wait_recv()
    out[...] = (
        mine[at.y].astype(F32) + y_second[0].astype(F32) + y_second[1].astype(F32)
    ).astype(BF16)


def scatter_line(net, acc, zz, up, down, z_first, z_next, out, cut):
    low, high = pl.ds(0, cut), pl.ds(cut, cut)
    p = net.put(acc.at[zz(4), low], z_first.at[0], seq=up)
    m = net.put(acc.at[zz(4), high], z_first.at[1], seq=down)
    yield
    p.wait_recv()
    m.wait_recv()
    add_into(acc.at[zz(3), low], z_first.at[0])
    add_into(acc.at[zz(-3), high], z_first.at[1])
    for i in (3, 2, 1):
        p = net.put(acc.at[zz(i)], z_next.at[i - 1, 0], seq=up)
        m = net.put(acc.at[zz(-i)], z_next.at[i - 1, 1], seq=down)
        yield
        p.wait_recv()
        m.wait_recv()
        if i > 1:
            add_into(acc.at[zz(i - 1)], z_next.at[i - 1, 0])
            add_into(acc.at[zz(1 - i)], z_next.at[i - 1, 1])
    total = acc[zz(0)].astype(F32) + z_next[0, 0].astype(F32) + z_next[0, 1].astype(F32)
    if out is None:
        acc[zz(0)] = total.astype(BF16)
    else:
        out[...] = total.astype(BF16)


def front_kernel(
    pooled, pool_out, gain, cot, wq, wk, wv, wo,
    q, g, kv, patches, wq_all,
    part, normed, cots, first, second, acc, wk_v, wv_v, wo_v, send, recv, local,
):
    at = Place()
    net = Net(send, recv)
    loads = [
        pltpu.make_async_copy(src, dst, local.at[i])
        for i, (src, dst) in enumerate(((wk, wk_v), (wv, wv_v), (wo, wo_v)))
    ]
    for load in loads:
        load.start()
    cots[at.t] = cot[...]
    wq_all[at.z, at.y, at.c] = wq[...].reshape(2, 32, GROUP * HD)
    greet(ring_partners(at) + line_partners(at))

    def own(total):
        rows = total.astype(BF16)
        patches[...] = rows
        hidden = rows.astype(F32)
        inv = lax.rsqrt(jnp.mean(hidden * hidden, -1, keepdims=True) + EPS)
        normed[at.t] = (hidden * inv * gain[...].astype(F32)).astype(BF16)

    def patch_chain():
        for i in range(8):
            cols = pl.ds(i * 512, 512)
            part[:, :, cols] = mm(pooled[...], pool_out[:, cols]).astype(BF16).reshape(NX, OWN, 512)
        yield from scatter_x(net, at, part, first, second, own)
        yield from gather_x(net, at, normed)

    wide = [gather_zy(net, at, wq_all), gather_yz(net, at, wq_all)]
    for chain in wide:
        next(chain)
    run([patch_chain(), gather_x(net, at, cots)] + wide)

    for load in loads:
        load.wait()

    def dot_loop(step):
        acc[...] = jnp.zeros_like(acc)

        @pl.loop(0, 8)
        def _(i):
            acc[...] += step(i)

    def columns(i):
        return pl.ds(pl.multiple_of(i * 512, 512), 512)

    def normed_cols(i):
        return normed[:, :, columns(i)].reshape(ROWS, 512)

    dot_loop(lambda i: mm(normed_cols(i), wq_all[i].reshape(512, GROUP * HD)))
    q[...] = acc[...].astype(BF16)
    dot_loop(lambda i: dg(cots[:, :, columns(i)].reshape(ROWS, 512), wo_v[:, columns(i)], NT))
    g[...] = acc[...].astype(BF16)

    acc[...] = jnp.zeros_like(acc)

    @pl.loop(0, 8)
    def _(i):
        rows = normed_cols(i)
        acc[:, 0:HD] += mm(rows, wk_v[columns(i), :])
        acc[:, HD:2 * HD] += mm(rows, wv_v[columns(i), :])

    kv[0] = acc[:, 0:HD].astype(BF16)
    kv[1] = acc[:, HD:2 * HD].astype(BF16)
    net.finish()


def spread_kernel(q, g, kv, kv_all, qb, gb, send, recv):
    at = Place()
    net = Net(send, recv)
    kv_all[at.z, at.y, at.c] = kv[...]
    greet(ring_partners(at) + [{"seq": at.twin}])
    chains = [gather_zy(net, at, kv_all), gather_yz(net, at, kv_all)]
    for chain in chains:
        next(chain)
    swaps = [
        net.put(q.at[pl.ds(HALF, HALF)], qb, seq=at.twin),
        net.put(g.at[pl.ds(HALF, HALF)], gb, seq=at.twin),
    ]
    run(chains)
    for copy in swaps:
        copy.wait_recv()
    net.finish()


def attend_kernel(q, g, qb, gb, kv, oa, ob, dqa, dqb, part, dk, dv):
    s = lax.axis_index("seq")
    rows = GROUP * HALF
    scale = HD ** (-0.5)
    c2 = scale * math.log2(math.e)
    groups = KB // HD
    dk[...] = jnp.zeros_like(dk)
    dv[...] = jnp.zeros_like(dv)

    def stack(ref):
        block = ref[0:HALF, :]
        return jnp.concatenate([block[:, h * HD:(h + 1) * HD] for h in range(GROUP)], 0)

    def unstack(value):
        return jnp.concatenate([value[h * HALF:(h + 1) * HALF] for h in range(GROUP)], 1)

    for q_ref, g_ref, o_ref, dq_ref, base in (
        (q, g, oa, dqa, s * ROWS),
        (qb, gb, ob, dqb, (SHARDS - 1 - s) * ROWS + HALF),
    ):
        qs, gs = stack(q_ref), stack(g_ref)
        qt = qs.T
        gt = gs.T
        pos = base + lax.rem(lax.broadcasted_iota(jnp.int32, (KB, rows), 1), HALF)
        key = lax.broadcasted_iota(jnp.int32, (KB, rows), 0)
        full = lax.div(base, KB)

        def block(j, which):
            return kv[pl.ds(j * groups, groups), which].reshape(KB, HD)

        def scores(j, masked):
            st = mm(block(j, 0), qt) * c2
            if masked:
                st = jnp.where(key + j * KB <= pos, st, NEG)
            return st

        def forward(j, carry, masked):
            top, mass, acc = carry
            st = scores(j, masked)
            new = jnp.maximum(top, jnp.max(st, 0, keepdims=True))
            fade = jnp.exp2(top - new)
            p = jnp.exp2(st - new)
            mass = mass * fade + jnp.sum(p, 0, keepdims=True)
            acc = acc * fade + dg(block(j, 1), p.astype(BF16), TN)
            return new, mass, acc

        carry = (
            jnp.full((1, rows), NEG, F32),
            jnp.zeros((1, rows), F32),
            jnp.zeros((HD, rows), F32),
        )
        carry = lax.fori_loop(0, full, lambda j, c: forward(j, c, False), carry)
        top, mass, acc = forward(full, carry, True)
        lse = top + jnp.log2(mass)
        ot = (acc / mass).astype(BF16)
        o_ref[...] = unstack(ot.T)
        delta = jnp.sum(gt.astype(F32) * ot.astype(F32), 0, keepdims=True)

        def backward(j, dqt, masked):
            prob = jnp.exp2(scores(j, masked) - lse)
            dprob = mm(block(j, 1), gt)
            ds = (prob * (dprob - delta)).astype(BF16)
            at = pl.ds(j * groups, groups)
            dk[at] += mm(ds, qs).reshape(groups, HD, HD)
            dv[at] += mm(prob.astype(BF16), gs).reshape(groups, HD, HD)
            return dqt + dg(block(j, 0), ds, TN)

        dqt = jnp.zeros((HD, rows), F32)
        dqt = lax.fori_loop(0, full, lambda j, c: backward(j, c, False), dqt)
        dqt = backward(full, dqt, True)
        dq_ref[...] = unstack((dqt * scale).T.astype(BF16))

    @pl.loop(0, SHARDS)
    def _(j):
        part[j, 0] = (dk[j] * scale).astype(BF16)
        part[j, 1] = dv[j].astype(BF16)


def collect_kernel(
    part, oa, ob, dqa, dqb, attn, dq, dkv,
    sib, acc0, acc1, ya1, ya2, za1, za2, yb1, yb2, zb1, zb2, send, recv,
):
    at = Place()
    net = Net(send, recv)
    attn[0:HALF, :] = oa[...]
    dq[0:HALF, :] = dqa[...]
    greet(ring_partners(at) + [{"seq": at.twin}])
    near = [
        net.put(part.at[pl.ds(0, NZ), pl.ds(0, NY), 1 - at.c, half], sib.at[half], seq=at.sib)
        for half in (1, 0)
    ]
    swaps = [
        net.put(ob, attn.at[pl.ds(HALF, HALF)], seq=at.twin),
        net.put(dqb, dq.at[pl.ds(HALF, HALF)], seq=at.twin),
    ]
    near[0].wait_recv()

    @pl.loop(0, NZ)
    def _(i):
        acc1[i] = (part[i, :, at.c, 1].astype(F32) + sib[1, i].astype(F32)).astype(BF16)

    later = scatter_zy(net, at, acc1, zb1, zb2, yb1, yb2, dkv.at[1])
    next(later)
    near[1].wait_recv()

    @pl.loop(0, NZ)
    def _(i):
        acc0[:, i] = (part[i, :, at.c, 0].astype(F32) + sib[0, i].astype(F32)).astype(BF16)

    run([scatter_yz(net, at, acc0, ya1, ya2, za1, za2, dkv.at[0]), later])
    for copy in swaps:
        copy.wait_recv()
    net.finish()


def back_kernel(
    attn, dq, dkv, patches, cot, gain, wq, wk, wv, wo,
    layer, grad,
    part, part2, first, second, first2, second2, wq_v, wk_v, wv_v, wo_v, send, recv, local,
):
    at = Place()
    net = Net(send, recv)
    loads = [
        pltpu.make_async_copy(src, dst, local.at[i])
        for i, (src, dst) in enumerate(((wo, wo_v), (wq, wq_v), (wk, wk_v), (wv, wv_v)))
    ]
    for load in loads:
        load.start()
    greet(line_partners(at))
    loads[0].wait()

    @pl.loop(0, 8)
    def _(i):
        cols = pl.ds(pl.multiple_of(i * 512, 512), 512)
        part[:, :, cols] = mm(attn[...], wo_v[:, cols]).astype(BF16).reshape(NX, OWN, 512)

    def layer_result(total):
        layer[...] = (patches[...].astype(F32) + total).astype(BF16)

    def grad_result(total):
        hidden = patches[...].astype(F32)
        inv = lax.rsqrt(jnp.mean(hidden * hidden, -1, keepdims=True) + EPS)
        unit = hidden * inv
        scaled = total * gain[...].astype(F32)
        mean = jnp.mean(scaled * unit, -1, keepdims=True)
        grad[...] = (cot[...].astype(F32) + inv * (scaled - unit * mean)).astype(BF16)

    out_chain = scatter_x(net, at, part, first, second, layer_result)
    next(out_chain)
    for load in loads[1:]:
        load.wait()

    @pl.loop(0, 8)
    def _(i):
        rows = pl.ds(pl.multiple_of(i * 512, 512), 512)
        total = dg(dq[...], wq_v[rows, :], NT)
        total = total + dg(dkv[0], wk_v[rows, :], NT) + dg(dkv[1], wv_v[rows, :], NT)
        part2[:, :, rows] = total.astype(BF16).reshape(NX, OWN, 512)

    run([scatter_x(net, at, part2, first2, second2, grad_result), out_chain])
    net.finish()


def pool_group(byte_block, lengths, pool_query, pool_key, pool_value):
    ends = jnp.cumsum(lengths)
    starts = ends - lengths
    where_at = jnp.arange(byte_block.shape[0], dtype=jnp.int32)
    member = (where_at[None, :] >= starts[:, None]) & (where_at[None, :] < ends[:, None])
    sums = mm(member.astype(BF16), byte_block)
    means = (sums / lengths[:, None].astype(F32)).astype(BF16)
    pool_q = mm(means, pool_query).astype(BF16)
    pool_k = mm(byte_block, pool_key).astype(BF16)
    pool_v = mm(byte_block, pool_value).astype(BF16)
    heads = pool_query.shape[1] // HD
    q_heads = pool_q.reshape(-1, heads, HD)
    k_heads = pool_k.reshape(-1, heads, HD)
    v_heads = pool_v.reshape(-1, heads, HD)
    scores = jnp.einsum("phd,bhd->hpb", q_heads, k_heads, preferred_element_type=F32)
    scores = jnp.where(member[None], scores * HD ** (-0.5), NEG)
    top = jnp.max(scores, -1, keepdims=True)
    expo = jnp.exp(scores - top)
    weights = (expo / jnp.sum(expo, -1, keepdims=True)).astype(BF16)
    pooled = jnp.einsum("hpb,bhd->phd", weights, v_heads, preferred_element_type=F32)
    return pooled.reshape(lengths.shape[0], -1).astype(BF16)


def sds(*shape):
    return jax.ShapeDtypeStruct(shape, BF16)


def buf(*shape):
    return pltpu.VMEM(shape, BF16)


def call(kernel, outs, specs, scratch, collective_id, flops, copies=0, local=0):
    sems = []
    if copies:
        sems = [pltpu.SemaphoreType.DMA((copies,)), pltpu.SemaphoreType.DMA((copies,))]
    if local:
        sems.append(pltpu.SemaphoreType.DMA((local,)))
    here, there = pl.BlockSpec(memory_space=pltpu.VMEM), pl.BlockSpec(memory_space=pl.ANY)
    return pl.pallas_call(
        kernel,
        out_shape=outs,
        in_specs=[here if c == "v" else there for c in specs],
        out_specs=[here] * len(outs),
        scratch_shapes=list(scratch) + sems,
        compiler_params=pltpu.CompilerParams(
            collective_id=collective_id,
            has_side_effects=collective_id is not None,
            vmem_limit_bytes=VMEM,
        ),
        cost_estimate=pl.CostEstimate(flops=flops, bytes_accessed=1 << 23, transcendentals=0),
    )


def front(pooled, pool_out, gain, cot, wq, wk, wv, wo):
    wide = GROUP * HD
    return call(
        front_kernel,
        [sds(ROWS, wide), sds(ROWS, wide), sds(2, ROWS, HD), sds(OWN, D), sds(NZ, NY, 2, 2, 32, wide)],
        "vvvvvaaa",
        [
            buf(NX, OWN, D), buf(NX, OWN, D), buf(NX, OWN, D), buf(2, OWN // 2, D), buf(2, OWN, D),
            pltpu.VMEM((ROWS, wide), F32), buf(D, HD), buf(D, HD), buf(wide, D),
        ],
        1, 2 * 10**9, 64, 3,
    )(pooled, pool_out, gain, cot, wq, wk, wv, wo)


def spread(q, g, kv):
    wide = GROUP * HD
    return call(
        spread_kernel,
        [sds(NZ, NY, 2, 2, ROWS, HD), sds(HALF, wide), sds(HALF, wide)],
        "vvv", [], 2, 10**6, 48,
    )(q, g, kv)


def attend(q, g, qb, gb, kv_all):
    wide = GROUP * HD
    return call(
        attend_kernel,
        [sds(HALF, wide)] * 4 + [sds(SHARDS, 2, ROWS, HD)],
        "vvvvv",
        [pltpu.VMEM((SHARDS, ROWS, HD), F32)] * 2,
        None, 4 * 10**9,
    )(q, g, qb, gb, kv_all)


def collect(part, oa, ob, dqa, dqb):
    wide = GROUP * HD
    half = ROWS // 2
    return call(
        collect_kernel,
        [sds(ROWS, wide), sds(ROWS, wide), sds(2, ROWS, HD)],
        "vvvvv",
        [
            buf(2, NZ, NY, ROWS, HD), buf(NY, NZ, ROWS, HD), buf(NZ, NY, ROWS, HD),
            buf(2, 4, ROWS, HD), buf(2, NZ, ROWS, HD),
            buf(2, half, HD), buf(3, 2, ROWS, HD),
            buf(2, half, HD), buf(2, ROWS, HD),
            buf(2, NY // 2, ROWS, HD), buf(3, 2, NY, ROWS, HD),
        ],
        3, 10**7, 48,
    )(part, oa, ob, dqa, dqb)


def back(attn, dq, dkv, patches, cot, gain, wq, wk, wv, wo):
    wide = GROUP * HD
    return call(
        back_kernel,
        [sds(OWN, D), sds(OWN, D)],
        "vvvvvvaaaa",
        [
            buf(NX, OWN, D), buf(NX, OWN, D), buf(2, OWN // 2, D), buf(2, OWN, D),
            buf(2, OWN // 2, D), buf(2, OWN, D),
            buf(D, wide), buf(D, HD), buf(D, HD), buf(wide, D),
        ],
        4, 2 * 10**9, 16, 4,
    )(attn, dq, dkv, patches, cot, gain, wq, wk, wv, wo)


def on_device(
    byte_rows,
    patch_lengths,
    pool_query,
    pool_key,
    pool_value,
    pool_out,
    norm_gain,
    query_weight,
    key_weight,
    value_weight,
    out_weight,
    cotangent,
):
    pooled = pool_group(byte_rows, patch_lengths[0], pool_query, pool_key, pool_value)
    gain = norm_gain.reshape(1, D)
    q, g, kv, patches, wq_all = front(
        pooled, pool_out, gain, cotangent, query_weight, key_weight, value_weight, out_weight
    )
    kv_all, qb, gb = spread(q, g, kv)
    oa, ob, dqa, dqb, part = attend(q, g, qb, gb, kv_all.reshape(SHARDS, 2, ROWS, HD))
    attn, dq, dkv = collect(part.reshape(NZ, NY, 2, 2, ROWS, HD), oa, ob, dqa, dqb)
    return tuple(
        back(
            attn, dq, dkv, patches, cotangent, gain,
            wq_all.reshape(D, GROUP * HD), key_weight, value_weight, out_weight,
        )
    )


def solution(mesh):
    placed = (
        P("seq", None),
        P("seq", None),
        P(None, "tensor"),
        P(None, "tensor"),
        P(None, "tensor"),
        P("tensor", None),
        P(),
        P("seq", "tensor"),
        P(None, "tensor"),
        P(None, "tensor"),
        P("tensor", None),
        P(("seq", "tensor"), None),
    )
    return jax.shard_map(
        on_device,
        mesh=mesh,
        in_specs=placed,
        out_specs=(P(("seq", "tensor"), None), P(("seq", "tensor"), None)),
        check_vma=False,
    )
```

```python
import math

import jax
import jax.numpy as jnp
from jax import lax
from jax.experimental import pallas as pl
from jax.experimental.pallas import tpu as pltpu
from jax.sharding import PartitionSpec as P

EPS = 1e-05
NEG = -1e30
MESH = pl.DeviceIdType.MESH
NZ, NY, NX = 8, 4, 4
HD = 128
GROUP = 4
ROWS = 128
HALF = 64
SHARDS = 64
D = 4096
OWN = 32
KB = 512
VMEM = 56 * 1024 * 1024
F32 = jnp.float32
BF16 = jnp.bfloat16
NT = (((1,), (1,)), ((), ()))
TN = (((0,), (0,)), ((), ()))


def mm(a, b):
    return jnp.dot(a, b, preferred_element_type=F32)


def dg(a, b, dims):
    return lax.dot_general(a, b, dims, preferred_element_type=F32)


class Place:
    def __init__(self):
        s = lax.axis_index("seq")
        self.s = s
        self.z = lax.div(s, 8)
        self.y = lax.rem(lax.div(s, 2), 4)
        self.c = lax.rem(s, 2)
        self.t = lax.axis_index("tensor")
        self.sib = self.seq(self.z, self.y, 1 - self.c)
        self.up = self.seq(self.zz(1), self.y, self.c)
        self.down = self.seq(self.zz(-1), self.y, self.c)
        self.north = self.seq(self.z, self.yy(1), self.c)
        self.south = self.seq(self.z, self.yy(-1), self.c)
        self.twin = SHARDS - 1 - s

    def zz(self, i):
        return lax.rem(self.z + NZ + i, NZ)

    def yy(self, i):
        return lax.rem(self.y + NY + i, NY)

    def tt(self, i):
        return lax.rem(self.t + NX + i, NX)

    def seq(self, z, y, c):
        return (z * NY + y) * 2 + c


class Net:
    def __init__(self, send, recv):
        self.send, self.recv, self.all = send, recv, []

    def put(self, src, dst, **device):
        n = len(self.all)
        copy = pltpu.make_async_remote_copy(
            src_ref=src,
            dst_ref=dst,
            send_sem=self.send.at[n],
            recv_sem=self.recv.at[n],
            device_id=device,
            device_id_type=MESH,
        )
        copy.start()
        self.all.append(copy)
        return copy

    def finish(self):
        for copy in self.all:
            copy.wait_send()


def greet(devices):
    barrier = pltpu.get_barrier_semaphore()
    for device in devices:
        pl.semaphore_signal(barrier, inc=1, device_id=device, device_id_type=MESH)
    pl.semaphore_wait(barrier, len(devices))


def partners(at):
    ring = [{"seq": d} for d in (at.sib, at.up, at.down, at.north, at.south, at.twin)]
    return ring + [{"tensor": at.tt(1)}, {"tensor": at.tt(-1)}]


def run(chains):
    chains = list(chains)
    while chains:
        left = []
        for chain in chains:
            try:
                next(chain)
                left.append(chain)
            except StopIteration:
                pass
        chains = left


def same(net, view, **device):
    return net.put(view, view, **device)


def gather_zy(net, at, buf):
    rows = buf.shape[4] // 2
    zz, yy, c, y = at.zz, at.yy, at.c, at.y
    for i in range(1, 4):
        p = same(net, buf.at[0, zz(1 - i), y, c], seq=at.up)
        m = same(net, buf.at[0, zz(i - 1), y, c], seq=at.down)
        yield
        p.wait_recv()
        m.wait_recv()
    p = same(net, buf.at[0, zz(-3), y, c, pl.ds(0, rows)], seq=at.up)
    m = same(net, buf.at[0, zz(3), y, c, pl.ds(rows, rows)], seq=at.down)
    yield
    p.wait_recv()
    m.wait_recv()
    every = pl.ds(0, NZ)
    p = same(net, buf.at[0, every, y, c], seq=at.north)
    m = same(net, buf.at[0, every, y, c], seq=at.south)
    sib = [same(net, buf.at[0, every, y, c], seq=at.sib)]
    yield
    p.wait_recv()
    m.wait_recv()
    p = same(net, buf.at[0, pl.ds(0, 4), yy(-1), c], seq=at.north)
    m = same(net, buf.at[0, pl.ds(4, 4), yy(1), c], seq=at.south)
    sib.append(same(net, buf.at[0, every, yy(-1), c], seq=at.sib))
    sib.append(same(net, buf.at[0, every, yy(1), c], seq=at.sib))
    yield
    p.wait_recv()
    m.wait_recv()
    sib.append(same(net, buf.at[0, every, yy(2), c], seq=at.sib))
    yield
    for copy in sib:
        copy.wait_recv()


def gather_yz(net, at, buf):
    rows = buf.shape[4] // 2
    zz, yy, c, z = at.zz, at.yy, at.c, at.z
    p = same(net, buf.at[1, z, at.y, c], seq=at.north)
    m = same(net, buf.at[1, z, at.y, c], seq=at.south)
    yield ()
    p.wait_recv()
    m.wait_recv()
    p = same(net, buf.at[1, z, yy(-1), c, pl.ds(0, rows)], seq=at.north)
    m = same(net, buf.at[1, z, yy(1), c, pl.ds(rows, rows)], seq=at.south)
    yield ()
    p.wait_recv()
    m.wait_recv()
    every = pl.ds(0, NY)
    sib, offsets = [same(net, buf.at[1, z, every, c], seq=at.sib)], (0,)
    for i in range(1, 5):
        if i < 4:
            p = same(net, buf.at[1, zz(1 - i), every, c], seq=at.up)
            m = same(net, buf.at[1, zz(i - 1), every, c], seq=at.down)
        else:
            p = same(net, buf.at[1, zz(-3), pl.ds(0, 2), c], seq=at.up)
            m = same(net, buf.at[1, zz(3), pl.ds(2, 2), c], seq=at.down)
        for copy in sib:
            copy.wait_recv()
        yield offsets
        p.wait_recv()
        m.wait_recv()
        offsets = (i, -i) if i < 4 else (4,)
        sib = [same(net, buf.at[1, zz(o), every, c], seq=at.sib) for o in offsets]
    yield ()
    for copy in sib:
        copy.wait_recv()
    yield offsets


def gather_x(net, at, buf, row):
    tt = at.tt
    rows, low, high = pl.ds(row, 16), pl.ds(0, D // 2), pl.ds(D // 2, D // 2)
    p = same(net, buf.at[at.t, rows], tensor=tt(1))
    m = same(net, buf.at[at.t, rows], tensor=tt(-1))
    yield
    p.wait_recv()
    m.wait_recv()
    p = same(net, buf.at[tt(-1), rows, low], tensor=tt(1))
    m = same(net, buf.at[tt(1), rows, high], tensor=tt(-1))
    yield
    p.wait_recv()
    m.wait_recv()


def add_into(ref, *others):
    total = ref[...].astype(F32)
    for other in others:
        total = total + other[...].astype(F32)
    ref[...] = total.astype(BF16)


def scatter_x(net, at, part, row, first, second, result):
    tt = at.tt
    rows, low, high = pl.ds(row, 16), pl.ds(0, D // 2), pl.ds(D // 2, D // 2)
    p = net.put(part.at[tt(2), rows, low], first.at[0], tensor=tt(1))
    m = net.put(part.at[tt(2), rows, high], first.at[1], tensor=tt(-1))
    yield
    p.wait_recv()
    add_into(part.at[tt(1), rows, low], first.at[0])
    p = net.put(part.at[tt(1), rows], second.at[0], tensor=tt(1))
    m.wait_recv()
    add_into(part.at[tt(-1), rows, high], first.at[1])
    m = net.put(part.at[tt(-1), rows], second.at[1], tensor=tt(-1))
    yield
    p.wait_recv()
    m.wait_recv()
    mine = part[at.t, rows, :].astype(F32)
    result(row, mine + second[0].astype(F32) + second[1].astype(F32))


def scatter_yz(net, at, part, sib, acc, y_first, y_second, z_first, z_next, out):
    yy, zz = at.yy, at.zz
    low, high = pl.ds(0, 4), pl.ds(4, 4)
    order = (yy(2), yy(1), yy(-1), yy(0))
    near = [
        net.put(part.at[0, pl.ds(0, NZ), y, 1 - at.c], sib.at[y], seq=at.sib) for y in order
    ]
    yield

    def own(k):
        near[k].wait_recv()
        y = order[k]
        acc[y] = (part[0, :, y, at.c].astype(F32) + sib[y].astype(F32)).astype(BF16)

    own(0)
    p = net.put(acc.at[yy(2), low], y_first.at[0], seq=at.north)
    m = net.put(acc.at[yy(2), high], y_first.at[1], seq=at.south)
    own(1)
    own(2)
    yield
    p.wait_recv()
    add_into(acc.at[yy(1), low], y_first.at[0])
    p = net.put(acc.at[yy(1)], y_second.at[0], seq=at.north)
    m.wait_recv()
    add_into(acc.at[yy(-1), high], y_first.at[1])
    m = net.put(acc.at[yy(-1)], y_second.at[1], seq=at.south)
    own(3)
    yield
    p.wait_recv()
    m.wait_recv()
    add_into(acc.at[at.y], y_second.at[0], y_second.at[1])
    mine = acc.at[at.y]
    low, high = pl.ds(0, 1), pl.ds(1, 1)
    p = net.put(mine.at[zz(4), low], z_first.at[0], seq=at.up)
    m = net.put(mine.at[zz(4), high], z_first.at[1], seq=at.down)
    yield
    p.wait_recv()
    m.wait_recv()
    add_into(mine.at[zz(3), low], z_first.at[0])
    add_into(mine.at[zz(-3), high], z_first.at[1])
    for i in (3, 2, 1):
        p = net.put(mine.at[zz(i)], z_next.at[i - 1, 0], seq=at.up)
        m = net.put(mine.at[zz(-i)], z_next.at[i - 1, 1], seq=at.down)
        yield
        p.wait_recv()
        m.wait_recv()
        if i > 1:
            add_into(mine.at[zz(i - 1)], z_next.at[i - 1, 0])
            add_into(mine.at[zz(1 - i)], z_next.at[i - 1, 1])
    total = mine[at.z].astype(F32) + z_next[0, 0].astype(F32) + z_next[0, 1].astype(F32)
    out(0, total)


def scatter_zy(net, at, part, sib, acc, z_first, z_next, y_first, y_second, out):
    zz, yy = at.zz, at.yy
    every = pl.ds(0, NY)
    low, high = pl.ds(0, 2), pl.ds(2, 2)

    def share(*offsets):
        return [
            (o, net.put(part.at[1, zz(o), every, 1 - at.c], sib.at[zz(o)], seq=at.sib)) for o in offsets
        ]

    def own(near):
        for o, copy in near:
            copy.wait_recv()
            z = zz(o)
            acc[z] = (part[1, z, :, at.c].astype(F32) + sib[z].astype(F32)).astype(BF16)

    yield (4,)
    near = share(4)
    yield (3, -3)
    own(near)
    near = share(3, -3)
    p = net.put(acc.at[zz(4), low], z_first.at[0], seq=at.up)
    m = net.put(acc.at[zz(4), high], z_first.at[1], seq=at.down)
    for i in (3, 2, 1):
        yield (i - 1, 1 - i) if i > 1 else (0,)
        own(near)
        near = share(i - 1, 1 - i) if i > 1 else share(0)
        p.wait_recv()
        m.wait_recv()
        if i == 3:
            add_into(acc.at[zz(3), low], z_first.at[0])
            add_into(acc.at[zz(-3), high], z_first.at[1])
        else:
            add_into(acc.at[zz(i)], z_next.at[i, 0])
            add_into(acc.at[zz(-i)], z_next.at[i, 1])
        p = net.put(acc.at[zz(i)], z_next.at[i - 1, 0], seq=at.up)
        m = net.put(acc.at[zz(-i)], z_next.at[i - 1, 1], seq=at.down)
    yield ()
    own(near)
    p.wait_recv()
    m.wait_recv()
    mine = acc.at[at.z]
    add_into(mine, z_next.at[0, 0], z_next.at[0, 1])
    p = net.put(mine.at[yy(2), pl.ds(0, 1)], y_first.at[0], seq=at.north)
    m = net.put(mine.at[yy(2), pl.ds(1, 1)], y_first.at[1], seq=at.south)
    yield ()
    p.wait_recv()
    m.wait_recv()
    add_into(mine.at[yy(1), pl.ds(0, 1)], y_first.at[0])
    add_into(mine.at[yy(-1), pl.ds(1, 1)], y_first.at[1])
    p = net.put(mine.at[yy(1)], y_second.at[0], seq=at.north)
    m = net.put(mine.at[yy(-1)], y_second.at[1], seq=at.south)
    yield ()
    p.wait_recv()
    m.wait_recv()
    out(1, mine[at.y].astype(F32) + y_second[0].astype(F32) + y_second[1].astype(F32))


def pool(lengths, byte, pool_query, pool_key, pool_value):
    nb = byte.shape[0]
    count = lengths[...].astype(F32)
    row = lax.broadcasted_iota(jnp.int32, (ROWS, ROWS), 0)
    col = lax.broadcasted_iota(jnp.int32, (ROWS, ROWS), 1)
    ends = jnp.sum(jnp.where(col <= row, count, 0.0), 1, keepdims=True)
    size = jnp.sum(jnp.where(col == row, count, 0.0), 1, keepdims=True)
    where_at = lax.broadcasted_iota(jnp.int32, (ROWS, nb), 1).astype(F32)
    member = (where_at >= ends - size) & (where_at < ends)
    sums = mm(jnp.where(member, 1.0, 0.0).astype(BF16), byte[...])
    means = (sums / size).astype(BF16)
    pq = mm(means, pool_query[...]).astype(BF16)
    pk = mm(byte[...], pool_key[...]).astype(BF16)
    pv = mm(byte[...], pool_value[...]).astype(BF16)
    heads = []
    for h in range(pq.shape[1] // HD):
        cols = slice(h * HD, (h + 1) * HD)
        scores = jnp.where(member, dg(pq[:, cols], pk[:, cols], NT) * HD ** (-0.5), NEG)
        expo = jnp.exp(scores - jnp.max(scores, -1, keepdims=True))
        weights = (expo / jnp.sum(expo, -1, keepdims=True)).astype(BF16)
        heads.append(mm(weights, pv[:, cols]))
    return jnp.concatenate(heads, 1).astype(BF16)


def stack(block):
    return jnp.concatenate([block[:, h * HD:(h + 1) * HD] for h in range(GROUP)], 0)


def unstack(value):
    return jnp.concatenate([value[h * HALF:(h + 1) * HALF] for h in range(GROUP)], 1)


def columns(i):
    return pl.ds(pl.multiple_of(i * 512, 512), 512)


def kernel(
    lengths, gain, byte_h, pq_h, pk_h, pv_h, po_h, wq_h, wk_h, wv_h, wo_h, cot_h,
    layer, grad,
    byte, pool_q, pool_k, pool_v, pool_o, wk, wv, wo, pooled, patches, normed, cots, wq,
    part, first, second, part2, first2, second2, part3, first3, second3, grad_acc,
    acc, q, g, qb, gb, attn, dq, ob, dqb,
    kvb, qs, qt, gs, gt, top, mass, oacc, lse, delta, dqt, dkv_acc, ahead,
    pgrad, sib0, sib1, acc0, acc1, ya1, ya2, za1, za2, yb1, yb2, zb1, zb2, dkv,
    send, recv, local,
):
    at = Place()
    net = Net(send, recv)
    c2 = HD ** (-0.5) * math.log2(math.e)
    loads = {}

    def load(name, src, dst):
        copy = pltpu.make_async_copy(src, dst, local.at[len(loads)])
        copy.start()
        loads[name] = copy

    def ready(*names):
        for name in names:
            loads[name].wait()

    for half in range(2):
        load("wq%d" % half, wq_h.at[pl.ds(half * 32, 32)], wq.at[half, at.z, at.y, at.c])
    load("byte", byte_h, byte)
    load("pq", pq_h, pool_q)
    load("pk", pk_h, pool_k)
    load("pv", pv_h, pool_v)
    load("po", po_h, pool_o)
    load("cot", cot_h, cots.at[at.t])
    load("wk", wk_h, wk)
    load("wv", wv_h, wv)
    load("wo", wo_h, wo)
    greet(partners(at))

    ready("wq0", "wq1")
    w0, w1 = gather_zy(net, at, wq), gather_yz(net, at, wq)
    next(w0)
    next(w1)

    ready("byte", "pq", "pk", "pv")
    pooled[...] = pool(lengths, byte, pool_q, pool_k, pool_v)
    next(w0)
    next(w1)
    ready("po")
    for i in range(8):
        cols = pl.ds(i * 512, 512)
        part[:, :, cols] = mm(pooled[...], pool_o[:, cols]).astype(BF16).reshape(NX, OWN, 512)

    def own(row, total):
        rows = total.astype(BF16)
        patches[pl.ds(row, 16), :] = rows
        hidden = rows.astype(F32)
        inv = lax.rsqrt(jnp.mean(hidden * hidden, -1, keepdims=True) + EPS)
        normed[at.t, pl.ds(row, 16), :] = (hidden * inv * gain[...].astype(F32)).astype(BF16)

    def patch_chain(k):
        yield from scatter_x(net, at, part, 16 * k, first.at[k], second.at[k], own)
        yield from gather_x(net, at, normed, 16 * k)

    run([patch_chain(0), patch_chain(1), w0, w1])

    def normed_cols(i):
        return normed[:, :, columns(i)].reshape(ROWS, 512)

    ready("wk", "wv", "cot", "wo")
    acc[...] = jnp.zeros_like(acc)

    @pl.loop(0, 8)
    def _(i):
        rows = normed_cols(i)
        acc[:, 0:HD] += mm(rows, wk[columns(i), :])
        acc[:, HD:2 * HD] += mm(rows, wv[columns(i), :])

    for half in range(2):
        for which in range(2):
            block = acc[half * HALF:(half + 1) * HALF, which * HD:(which + 1) * HD]
            kvb[half, at.z, at.y, at.c, which] = block.astype(BF16)
    k0, k1 = gather_zy(net, at, kvb), gather_yz(net, at, kvb)
    next(k1)
    next(k0)
    cot_chains = [gather_x(net, at, cots, 0), gather_x(net, at, cots, 16)]
    for chain in cot_chains:
        next(chain)

    acc[...] = jnp.zeros_like(acc)

    @pl.loop(0, 8)
    def _(i):
        w = jnp.concatenate([wq[half, i, y, c] for y in range(NY) for c in range(2) for half in range(2)], 0)
        acc[...] += mm(normed_cols(i), w)

    q[...] = acc[...].astype(BF16)
    q_swap = net.put(q.at[pl.ds(HALF, HALF)], qb, seq=at.twin)
    next(k1)
    next(k0)

    def prepare(st, block, straight, turned):
        straight[st] = stack(block)
        turned[st] = straight[st].T

    prepare(0, q[0:HALF, :], qs, qt)
    top[...] = jnp.full_like(top, NEG)
    mass[...] = jnp.zeros_like(mass)
    oacc[...] = jnp.zeros_like(oacc)
    for chain in cot_chains:
        next(chain)
    offsets = next(k1)
    next(k0)
    q_swap.wait_recv()
    prepare(1, qb[...], qs, qt)

    column = lax.broadcasted_iota(jnp.int32, (KB, GROUP * HALF), 1)
    key = lax.broadcasted_iota(jnp.int32, (KB, GROUP * HALF), 0)
    ahead[...] = (key >> 6) * ROWS + (key & (HALF - 1)) - (column & (HALF - 1))

    def keys(half, z, which):
        return kvb[half, z, :, :, which].reshape(KB, HD)

    def scores(half, z, st, masked):
        out = mm(keys(half, z, 0), qt[st]) * c2
        if masked:
            mine, other = lax.rem(at.s, 8) * ROWS, lax.rem(at.twin, 8) * ROWS + HALF
            base = mine + st * (other - mine) - half * HALF
            out = jnp.where(ahead[...] <= base, out, NEG)
        return out

    def forward(half, z, st, masked):
        out = scores(half, z, st, masked)
        old = top[st]
        new = jnp.maximum(old, jnp.max(out, 0, keepdims=True))
        fade = jnp.exp2(old - new)
        p = jnp.exp2(out - new)
        mass[st] = mass[st] * fade + jnp.sum(p, 0, keepdims=True)
        oacc[st] = oacc[st] * fade + dg(keys(half, z, 1), p.astype(BF16), TN)
        top[st] = new

    def backward(half, z, st, masked):
        prob = jnp.exp2(scores(half, z, st, masked) - lse[st])
        dprob = mm(keys(half, z, 1), gt[st])
        ds = (prob * (dprob - delta[st])).astype(BF16)
        dkv_acc[0] += mm(ds, qs[st])
        dkv_acc[1] += mm(prob.astype(BF16), gs[st])
        dqt[st] += dg(keys(half, z, 0), ds, TN)

    def tasks(body, half, z):
        @pl.loop(0, 2)
        def _(st):
            last = at.z + st * (NZ - 1 - 2 * at.z)

            @pl.when(z < last)
            def _():
                body(half, z, st, False)

            @pl.when(z == last)
            def _():
                body(half, z, st, True)

    def groups(body, offsets):
        if len(offsets) == 1:
            body(at.zz(offsets[0]))
        elif offsets:

            @pl.loop(0, 2)
            def _(k):
                body(at.zz(offsets[0] * (1 - 2 * k)))

    def forward_group(half, z):
        tasks(forward, half, z)

    steps = 0
    while offsets is not None:
        groups(lambda z: forward_group(1, z), offsets)
        if k0 is not None:
            try:
                next(k0)
            except StopIteration:
                k0 = None

                @pl.loop(0, NZ)
                def _(z):
                    forward_group(0, z)
        if steps == 0:
            for chain in cot_chains:
                next(chain, None)
            acc[...] = jnp.zeros_like(acc)

            @pl.loop(0, 8)
            def _(i):
                acc[...] += dg(cots[:, :, columns(i)].reshape(ROWS, 512), wo[:, columns(i)], NT)

            g[...] = acc[...].astype(BF16)
            g_swap = net.put(g.at[pl.ds(HALF, HALF)], gb, seq=at.twin)
        steps += 1
        offsets = next(k1, None)
    assert k0 is None

    prepare(0, g[0:HALF, :], gs, gt)
    g_swap.wait_recv()
    prepare(1, gb[...], gs, gt)
    for st in range(2):
        ot = (oacc[st] / mass[st]).astype(BF16)
        lse[st] = top[st] + jnp.log2(mass[st])
        delta[st] = jnp.sum(gt[st].astype(F32) * ot.astype(F32), 0, keepdims=True)
        if st == 0:
            attn[0:HALF, :] = unstack(ot.T)
        else:
            ob[...] = unstack(ot.T)
    o_swap = net.put(ob, attn.at[pl.ds(HALF, HALF)], seq=at.twin)
    dqt[...] = jnp.zeros_like(dqt)

    def backward_group(half, z):
        dkv_acc[...] = jnp.zeros_like(dkv_acc)
        tasks(backward, half, z)
        pgrad[half, z, :, :, 0] = (dkv_acc[0] * HD ** (-0.5)).astype(BF16).reshape(NY, 2, HALF, HD)
        pgrad[half, z, :, :, 1] = dkv_acc[1].astype(BF16).reshape(NY, 2, HALF, HD)

    @pl.loop(0, NZ)
    def _(z):
        backward_group(0, z)

    def out(half, total):
        dkv[0, pl.ds(half * HALF, HALF), :] = total[0].astype(BF16)
        dkv[1, pl.ds(half * HALF, HALF), :] = total[1].astype(BF16)

    r0 = scatter_yz(net, at, pgrad, sib0, acc0, ya1, ya2, za1, za2, out)
    next(r0)
    o_swap.wait_recv()

    @pl.loop(0, 8)
    def _(i):
        cols = columns(i)
        part2[:, :, cols] = mm(attn[...], wo[:, cols]).astype(BF16).reshape(NX, OWN, 512)

    def layer_result(row, total):
        rows = pl.ds(row, 16)
        layer[rows, :] = (patches[rows, :].astype(F32) + total).astype(BF16)

    lay = [scatter_x(net, at, part2, 16 * k, first2.at[k], second2.at[k], layer_result) for k in range(2)]
    for chain in lay:
        next(chain)
    r1 = scatter_zy(net, at, pgrad, sib1, acc1, zb1, zb2, yb1, yb2, out)
    computed = 0
    while computed < NZ:
        offsets = next(r1)
        groups(lambda z: backward_group(1, z), offsets)
        computed += len(offsets)
        next(r0, None)
        for chain in lay:
            next(chain, None)

    attn_dq = (dqt[0] * HD ** (-0.5)).T.astype(BF16)
    dq[0:HALF, :] = unstack(attn_dq)
    dqb[...] = unstack((dqt[1] * HD ** (-0.5)).T.astype(BF16))
    dq_swap = net.put(dqb, dq.at[pl.ds(HALF, HALF)], seq=at.twin)
    next(r1)
    next(r0, None)
    dq_swap.wait_recv()

    @pl.loop(0, 8)
    def _(i):
        w = jnp.concatenate([wq[half, i, y, c] for y in range(NY) for c in range(2) for half in range(2)], 0)
        grad_acc[:, columns(i)] = dg(dq[...], w, NT)

    run([r1, r0] + lay)

    @pl.loop(0, 8)
    def _(i):
        rows = columns(i)
        total = grad_acc[:, rows] + dg(dkv[0], wk[rows, :], NT) + dg(dkv[1], wv[rows, :], NT)
        part3[:, :, rows] = total.astype(BF16).reshape(NX, OWN, 512)

    def grad_result(row, total):
        rows = pl.ds(row, 16)
        hidden = patches[rows, :].astype(F32)
        inv = lax.rsqrt(jnp.mean(hidden * hidden, -1, keepdims=True) + EPS)
        unit = hidden * inv
        scaled = total * gain[...].astype(F32)
        mean = jnp.mean(scaled * unit, -1, keepdims=True)
        cot = cots[at.t, rows, :].astype(F32)
        grad[rows, :] = (cot + inv * (scaled - unit * mean)).astype(BF16)

    run([scatter_x(net, at, part3, 16 * k, first3.at[k], second3.at[k], grad_result) for k in range(2)])
    net.finish()


def buf(*shape):
    return pltpu.VMEM(shape, BF16)


def wide(*shape):
    return pltpu.VMEM(shape, F32)


def on_device(
    byte_rows,
    patch_lengths,
    pool_query,
    pool_key,
    pool_value,
    pool_out,
    norm_gain,
    query_weight,
    key_weight,
    value_weight,
    out_weight,
    cotangent,
):
    heads = GROUP * HD
    here, there = pl.BlockSpec(memory_space=pltpu.VMEM), pl.BlockSpec(memory_space=pl.ANY)
    line = [buf(NX, OWN, D), buf(2, 2, 16, D // 2), buf(2, 2, 16, D)]
    half = (2, HALF, HD)
    scratch = [
        buf(*byte_rows.shape), buf(*pool_query.shape), buf(*pool_key.shape), buf(*pool_value.shape),
        buf(*pool_out.shape), buf(*key_weight.shape), buf(*value_weight.shape), buf(*out_weight.shape),
        buf(ROWS, 2 * HD), buf(OWN, D), buf(NX, OWN, D), buf(NX, OWN, D), buf(2, NZ, NY, 2, 32, heads),
        *line, *line, *line, wide(ROWS, D),
        wide(ROWS, heads), buf(ROWS, heads), buf(ROWS, heads), buf(HALF, heads), buf(HALF, heads),
        buf(ROWS, heads), buf(ROWS, heads), buf(HALF, heads), buf(HALF, heads),
        buf(2, NZ, NY, 2, *half), buf(2, GROUP * HALF, HD), buf(2, HD, GROUP * HALF),
        buf(2, GROUP * HALF, HD), buf(2, HD, GROUP * HALF),
        wide(2, 1, GROUP * HALF), wide(2, 1, GROUP * HALF), wide(2, HD, GROUP * HALF),
        wide(2, 1, GROUP * HALF), wide(2, 1, GROUP * HALF), wide(2, HD, GROUP * HALF), wide(2, KB, HD), pltpu.VMEM((KB, GROUP * HALF), jnp.int32),
        buf(2, NZ, NY, 2, *half), buf(NY, NZ, *half), buf(NZ, NY, *half), buf(NY, NZ, *half), buf(NZ, NY, *half),
        buf(2, 4, *half), buf(2, NZ, *half), buf(2, 1, HALF, HD), buf(3, 2, *half),
        buf(2, 1, HALF, HD), buf(2, *half), buf(2, 2, *half), buf(3, 2, NY, *half),
        buf(2, ROWS, HD),
        pltpu.SemaphoreType.DMA((160,)), pltpu.SemaphoreType.DMA((160,)), pltpu.SemaphoreType.DMA((16,)),
    ]
    rows = jax.ShapeDtypeStruct((OWN, D), BF16)
    return tuple(
        pl.pallas_call(
            kernel,
            out_shape=[rows, rows],
            in_specs=[here] * 2 + [there] * 10,
            out_specs=[here] * 2,
            scratch_shapes=scratch,
            compiler_params=pltpu.CompilerParams(
                collective_id=1, has_side_effects=True, vmem_limit_bytes=VMEM
            ),
            cost_estimate=pl.CostEstimate(flops=10**10, bytes_accessed=1 << 24, transcendentals=0),
        )(
            patch_lengths, norm_gain.reshape(1, D), byte_rows, pool_query, pool_key, pool_value, pool_out,
            query_weight, key_weight, value_weight, out_weight, cotangent,
        )
    )


def solution(mesh):
    placed = (
        P("seq", None),
        P("seq", None),
        P(None, "tensor"),
        P(None, "tensor"),
        P(None, "tensor"),
        P("tensor", None),
        P(),
        P("seq", "tensor"),
        P(None, "tensor"),
        P(None, "tensor"),
        P("tensor", None),
        P(("seq", "tensor"), None),
    )
    return jax.shard_map(
        on_device,
        mesh=mesh,
        in_specs=placed,
        out_specs=(P(("seq", "tensor"), None), P(("seq", "tensor"), None)),
        check_vma=False,
    )
```

```python
import math

import jax
import jax.numpy as jnp
from jax import lax
from jax.experimental import pallas as pl
from jax.experimental.pallas import tpu as pltpu
from jax.sharding import PartitionSpec as P

EPS = 1e-05
NEG = -1e30
MESH = pl.DeviceIdType.MESH
NZ, NY, NX = 8, 4, 4
HD = 128
GROUP = 4
ROWS = 128
HALF = 64
SHARDS = 64
D = 4096
OWN = 32
KB = 512
VMEM = 56 * 1024 * 1024
F32 = jnp.float32
BF16 = jnp.bfloat16
NT = (((1,), (1,)), ((), ()))
TN = (((0,), (0,)), ((), ()))


def mm(a, b):
    return jnp.dot(a, b, preferred_element_type=F32)


def dg(a, b, dims):
    return lax.dot_general(a, b, dims, preferred_element_type=F32)


class Place:
    def __init__(self):
        s = lax.axis_index("seq")
        self.s = s
        self.z = lax.div(s, 8)
        self.y = lax.rem(lax.div(s, 2), 4)
        self.c = lax.rem(s, 2)
        self.t = lax.axis_index("tensor")
        self.sib = self.seq(self.z, self.y, 1 - self.c)
        self.up = self.seq(self.zz(1), self.y, self.c)
        self.down = self.seq(self.zz(-1), self.y, self.c)
        self.north = self.seq(self.z, self.yy(1), self.c)
        self.south = self.seq(self.z, self.yy(-1), self.c)
        self.across = self.seq(self.z, self.yy(2), self.c)
        self.twin = SHARDS - 1 - s

    def zz(self, i):
        return lax.rem(self.z + NZ + i, NZ)

    def yy(self, i):
        return lax.rem(self.y + NY + i, NY)

    def tt(self, i):
        return lax.rem(self.t + NX + i, NX)

    def seq(self, z, y, c):
        return (z * NY + y) * 2 + c


class Net:
    def __init__(self, send, recv):
        self.send, self.recv, self.all = send, recv, []

    def put(self, src, dst, **device):
        n = len(self.all)
        copy = pltpu.make_async_remote_copy(
            src_ref=src,
            dst_ref=dst,
            send_sem=self.send.at[n],
            recv_sem=self.recv.at[n],
            device_id=device,
            device_id_type=MESH,
        )
        copy.start()
        self.all.append(copy)
        return copy

    def finish(self):
        for copy in self.all:
            copy.wait_send()


def greet(devices):
    barrier = pltpu.get_barrier_semaphore()
    for device in devices:
        pl.semaphore_signal(barrier, inc=1, device_id=device, device_id_type=MESH)
    pl.semaphore_wait(barrier, len(devices))


def partners(at):
    ring = [{"seq": d} for d in (at.sib, at.up, at.down, at.north, at.south, at.across, at.twin)]
    return ring + [{"tensor": at.tt(1)}, {"tensor": at.tt(-1)}]


def run(chains):
    chains = list(chains)
    while chains:
        left = []
        for chain in chains:
            try:
                next(chain)
                left.append(chain)
            except StopIteration:
                pass
        chains = left


def same(net, view, **device):
    return net.put(view, view, **device)


def gather(net, at, buf):
    n = buf.shape[4] // 2
    zz, yy, c, y, z = at.zz, at.yy, at.c, at.y, at.z
    every, low, high = pl.ds(0, NY), pl.ds(0, n), pl.ds(n, n)

    def unit(o, j):
        return buf.at[0, zz(o), yy(j), c]

    def piece(o, j, rows):
        return buf.at[0, zz(o), yy(j), c, rows]

    def z_send(i):
        if i < 3:
            return [same(net, unit(-i, 0), seq=at.up), same(net, unit(i, 0), seq=at.down)]
        return [same(net, piece(-3, 0, low), seq=at.up), same(net, piece(3, 0, high), seq=at.down)]

    def y_send(*offsets):
        return [
            same(net, unit(o, 0), seq=to) for o in offsets for to in (at.north, at.south)
        ]

    def y_pass(*offsets):
        if len(offsets) == 1:
            o = offsets[0]
            return [same(net, piece(o, -1, low), seq=at.north), same(net, piece(o, 1, high), seq=at.south)]
        o, q = offsets
        return [same(net, unit(o, -1), seq=at.north), same(net, unit(q, 1), seq=at.south)]

    def got(copies):
        for copy in copies:
            copy.wait_recv()

    def group_send(i):
        pairs = []
        for k in range(2):
            pair = pl.ds(2 * k, 2)
            go = []
            if i < 3 or k == 0:
                go.append(same(net, buf.at[1, zz(-i), pair, c], seq=at.up))
            if i < 3 or k == 1:
                go.append(same(net, buf.at[1, zz(i), pair, c], seq=at.down))
            pairs.append(go)
        return pairs

    def group_pass(i, pairs):
        after = []
        for k in range(2):
            pair = pl.ds(2 * k, 2)
            got(pairs[k])
            go = []
            if i < 3 or k == 0:
                go.append(same(net, buf.at[1, zz(-i), pair, c], seq=at.up))
            if i < 3 or k == 1:
                go.append(same(net, buf.at[1, zz(i), pair, c], seq=at.down))
            after.append(go)
        return after

    def share(*offsets):
        return [same(net, buf.at[1, zz(o), every, c], seq=at.sib) for o in offsets]

    def share0(j):
        return same(net, buf.at[0, pl.ds(0, NZ), yy(j), c], seq=at.sib)

    mine = buf.at[1, z, y, c]
    first = [same(net, mine, seq=to) for to in (at.north, at.south, at.across)]
    zs = z_send(0)
    ys = [y_send(0)]
    yield ()
    got(first)
    pairs = group_send(0)
    sib = share(0)
    got(zs)
    zs = z_send(1)
    ys.append(y_send(1, -1))
    yield ()
    got(zs)
    zs = z_send(2)
    ys.append(y_send(2, -2))
    pairs = group_pass(1, pairs)
    got(sib)
    sib = share(1, -1)
    got(ys[0])
    passed = y_pass(0)
    yield (0,)
    got(zs)
    zs = z_send(3)
    ys.append(y_send(3, -3))
    pairs = group_pass(2, pairs)
    got(sib)
    sib = share(2, -2)
    got(ys[1])
    passed += y_pass(1, -1)
    yield (1, -1)
    got(zs)
    ys.append(y_send(4))
    pairs = group_pass(3, pairs)
    got(sib)
    sib = share(3, -3)
    sib0 = [share0(0)]
    got(ys[2])
    passed += y_pass(2, -2)
    yield (2, -2)
    got(ys[3])
    passed += y_pass(3, -3)
    got(pairs[0] + pairs[1])
    got(sib)
    sib = share(4)
    got(ys[4])
    passed += y_pass(4)
    sib0 += [share0(1), share0(-1)]
    yield (3, -3)
    got(passed)
    sib0.append(share0(2))
    got(sib)
    yield (4,)
    got(sib0)


def gather_x(net, at, buf, row):
    tt = at.tt
    rows, low, high = pl.ds(row, 16), pl.ds(0, D // 2), pl.ds(D // 2, D // 2)
    p = same(net, buf.at[at.t, rows], tensor=tt(1))
    m = same(net, buf.at[at.t, rows], tensor=tt(-1))
    yield
    p.wait_recv()
    m.wait_recv()
    p = same(net, buf.at[tt(-1), rows, low], tensor=tt(1))
    m = same(net, buf.at[tt(1), rows, high], tensor=tt(-1))
    yield
    p.wait_recv()
    m.wait_recv()


def add_into(ref, *others):
    total = ref[...].astype(F32)
    for other in others:
        total = total + other[...].astype(F32)
    ref[...] = total.astype(BF16)


def scatter_x(net, at, part, row, first, second, result):
    tt = at.tt
    rows, low, high = pl.ds(row, 16), pl.ds(0, D // 2), pl.ds(D // 2, D // 2)
    p = net.put(part.at[tt(2), rows, low], first.at[0], tensor=tt(1))
    m = net.put(part.at[tt(2), rows, high], first.at[1], tensor=tt(-1))
    yield
    p.wait_recv()
    add_into(part.at[tt(1), rows, low], first.at[0])
    p = net.put(part.at[tt(1), rows], second.at[0], tensor=tt(1))
    m.wait_recv()
    add_into(part.at[tt(-1), rows, high], first.at[1])
    m = net.put(part.at[tt(-1), rows], second.at[1], tensor=tt(-1))
    yield
    p.wait_recv()
    m.wait_recv()
    mine = part[at.t, rows, :].astype(F32)
    result(row, mine + second[0].astype(F32) + second[1].astype(F32))


def slot(o):
    return o % NZ


def scatter(net, at, part, sib, acc, y_first, y_next, za_first, za_next, zb_first, zb_next, y_last, out):
    zz, yy = at.zz, at.yy
    both, every = pl.ds(0, 2), pl.ds(0, NY)
    one, two = pl.ds(0, 1), pl.ds(1, 1)
    near, firsts, nexts, ring0, ring1 = {}, {}, {}, {}, {}

    def got(copies):
        for copy in copies:
            copy.wait_recv()

    def share(offsets):
        for o in offsets:
            near[o] = net.put(part.at[both, zz(o), every, 1 - at.c], sib.at[both, zz(o)], seq=at.sib)

    def own(offsets):
        for o in offsets:
            near[o].wait_recv()
            z = zz(o)
            acc[:, z] = (part[:, z, :, at.c].astype(F32) + sib[:, z].astype(F32)).astype(BF16)

    def y_one(offsets):
        for o in offsets:
            src, dst = acc.at[0, zz(o), yy(2)], y_first.at[slot(o)]
            if o in (0, 4):
                firsts[o] = [
                    net.put(src.at[one], dst.at[one], seq=at.north),
                    net.put(src.at[two], dst.at[two], seq=at.south),
                ]
            else:
                firsts[o] = [net.put(src, dst, seq=at.north if o > 0 else at.south)]

    def y_two(offsets):
        for o in offsets:
            got(firsts[o])
            z, came = zz(o), y_first.at[slot(o)]
            if o in (0, 4):
                add_into(acc.at[0, z, yy(1), one], came.at[one])
                add_into(acc.at[0, z, yy(-1), two], came.at[two])
            else:
                add_into(acc.at[0, z, yy(1 if o > 0 else -1)], came)
            nexts[o] = [
                net.put(acc.at[0, z, yy(1)], y_next.at[slot(o), 0], seq=at.north),
                net.put(acc.at[0, z, yy(-1)], y_next.at[slot(o), 1], seq=at.south),
            ]

    def y_done(offsets):
        for o in offsets:
            got(nexts[o])

    def z_zero(i):
        def total(o, *came):
            add_into(acc.at[0, zz(o), at.y], y_next.at[slot(o), 0], y_next.at[slot(o), 1], *came)

        if i == 4:
            total(4)
            src = acc.at[0, zz(4), at.y]
            ring0[4] = [
                net.put(src.at[one], za_first.at[one], seq=at.up),
                net.put(src.at[two], za_first.at[two], seq=at.down),
            ]
            return
        got(ring0[i + 1])
        if i == 0:
            block = acc[0, at.z, at.y].astype(F32)
            for came in (y_next.at[0, 0], y_next.at[0, 1], za_next.at[0, 0], za_next.at[0, 1]):
                block = block + came[...].astype(F32)
            out(0, block)
            return
        if i == 3:
            total(3)
            total(-3)
            add_into(acc.at[0, zz(3), at.y, one], za_first.at[one])
            add_into(acc.at[0, zz(-3), at.y, two], za_first.at[two])
        else:
            total(i, za_next.at[i, 0])
            total(-i, za_next.at[i, 1])
        ring0[i] = [
            net.put(acc.at[0, zz(i), at.y], za_next.at[i - 1, 0], seq=at.up),
            net.put(acc.at[0, zz(-i), at.y], za_next.at[i - 1, 1], seq=at.down),
        ]

    def z_one(i):
        low, high = pl.ds(0, 2), pl.ds(2, 2)
        if i == 4:
            ring1[4] = [
                net.put(acc.at[1, zz(4), low], zb_first.at[low], seq=at.up),
                net.put(acc.at[1, zz(4), high], zb_first.at[high], seq=at.down),
            ]
            return
        if i == 3:
            got(ring1[4])
            add_into(acc.at[1, zz(3), low], zb_first.at[low])
            add_into(acc.at[1, zz(-3), high], zb_first.at[high])
        go = []
        for k, pair in enumerate((low, high)):
            for side, o, to in ((0, i, at.up), (1, -i, at.down)):
                if i < 3:
                    ring1[i + 1][2 * k + side].wait_recv()
                    add_into(acc.at[1, zz(o), pair], zb_next.at[i, side, pair])
                go.append(net.put(acc.at[1, zz(o), pair], zb_next.at[i - 1, side, pair], seq=to))
        ring1[i] = go

    rounds = ((4,), (3, -3), (2, -2), (1, -1), (0,))
    yield rounds[0]
    share(rounds[0])
    yield rounds[1]
    share(rounds[1])
    own(rounds[0])
    z_one(4)
    y_one(rounds[0])
    yield rounds[2]
    share(rounds[2])
    own(rounds[1])
    z_one(3)
    y_one(rounds[1])
    y_two(rounds[0])
    yield rounds[3]
    share(rounds[3])
    own(rounds[2])
    z_one(2)
    y_one(rounds[2])
    y_two(rounds[1])
    y_done(rounds[0])
    z_zero(4)
    yield rounds[4]
    share(rounds[4])
    own(rounds[3])
    z_one(1)
    y_one(rounds[3])
    y_two(rounds[2])
    y_done(rounds[1])
    z_zero(3)
    yield ()
    own(rounds[4])
    y_one(rounds[4])
    y_two(rounds[3])
    y_done(rounds[2])
    z_zero(2)
    got(ring1[1])
    add_into(acc.at[1, at.z], zb_next.at[0, 0], zb_next.at[0, 1])
    last = [
        net.put(acc.at[1, at.z, yy(j)], y_last.at[k], seq=to)
        for k, (j, to) in enumerate(((2, at.across), (1, at.north), (-1, at.south)))
    ]
    yield ()
    y_two(rounds[4])
    y_done(rounds[3])
    z_zero(1)
    yield ()
    got(last)
    block = acc[1, at.z, at.y].astype(F32)
    for k in range(3):
        block = block + y_last[k].astype(F32)
    out(1, block)
    y_done(rounds[4])
    z_zero(0)


def pool(lengths, byte, pool_query, pool_key, pool_value):
    nb = byte.shape[0]
    count = lengths[...].astype(F32)
    row = lax.broadcasted_iota(jnp.int32, (ROWS, ROWS), 0)
    col = lax.broadcasted_iota(jnp.int32, (ROWS, ROWS), 1)
    ends = jnp.sum(jnp.where(col <= row, count, 0.0), 1, keepdims=True)
    size = jnp.sum(jnp.where(col == row, count, 0.0), 1, keepdims=True)
    where_at = lax.broadcasted_iota(jnp.int32, (ROWS, nb), 1).astype(F32)
    member = (where_at >= ends - size) & (where_at < ends)
    sums = mm(jnp.where(member, 1.0, 0.0).astype(BF16), byte[...])
    means = (sums / size).astype(BF16)
    pq = mm(means, pool_query[...]).astype(BF16)
    pk = mm(byte[...], pool_key[...]).astype(BF16)
    pv = mm(byte[...], pool_value[...]).astype(BF16)
    heads = []
    for h in range(pq.shape[1] // HD):
        cols = slice(h * HD, (h + 1) * HD)
        scores = jnp.where(member, dg(pq[:, cols], pk[:, cols], NT) * HD ** (-0.5), NEG)
        expo = jnp.exp(scores - jnp.max(scores, -1, keepdims=True))
        weights = (expo / jnp.sum(expo, -1, keepdims=True)).astype(BF16)
        heads.append(mm(weights, pv[:, cols]))
    return jnp.concatenate(heads, 1).astype(BF16)


def stack(block):
    return jnp.concatenate([block[:, h * HD:(h + 1) * HD] for h in range(GROUP)], 0)


def unstack(value):
    return jnp.concatenate([value[h * HALF:(h + 1) * HALF] for h in range(GROUP)], 1)


def columns(i):
    return pl.ds(pl.multiple_of(i * 512, 512), 512)


def kernel(
    lengths, gain, byte_h, pq_h, pk_h, pv_h, po_h, wq_h, wk_h, wv_h, wo_h, cot_h,
    layer, grad,
    byte, pool_q, pool_k, pool_v, pool_o, wk, wv, wo, pooled, patches, normed, cots, wq,
    part, first, second, part2, first2, second2, part3, first3, second3, grad_acc,
    acc, q, g, qb, gb, attn, dq, ob, dqb,
    kvb, qs, qt, gs, gt, top, mass, oacc, lse, delta, dqt, dkv_acc, ahead,
    pgrad, sib, gsum, y1, y2, za1, za2, zb1, zb2, y3, dkv,
    send, recv, local,
):
    at = Place()
    net = Net(send, recv)
    c2 = HD ** (-0.5) * math.log2(math.e)
    loads = {}

    def load(name, src, dst):
        copy = pltpu.make_async_copy(src, dst, local.at[len(loads)])
        copy.start()
        loads[name] = copy

    def ready(*names):
        for name in names:
            loads[name].wait()

    for half in range(2):
        load("wq%d" % half, wq_h.at[pl.ds(half * 32, 32)], wq.at[half, at.z, at.y, at.c])
    load("byte", byte_h, byte)
    load("pq", pq_h, pool_q)
    load("pk", pk_h, pool_k)
    load("pv", pv_h, pool_v)
    load("po", po_h, pool_o)
    load("cot", cot_h, cots.at[at.t])
    load("wk", wk_h, wk)
    load("wv", wv_h, wv)
    load("wo", wo_h, wo)
    greet(partners(at))

    ready("wq0", "wq1")
    weights = gather(net, at, wq)
    next(weights)

    ready("byte", "pq", "pk", "pv")
    pooled[...] = pool(lengths, byte, pool_q, pool_k, pool_v)
    next(weights)
    ready("po")
    for i in range(8):
        cols = pl.ds(i * 512, 512)
        part[:, :, cols] = mm(pooled[...], pool_o[:, cols]).astype(BF16).reshape(NX, OWN, 512)

    def own(row, total):
        rows = total.astype(BF16)
        patches[pl.ds(row, 16), :] = rows
        hidden = rows.astype(F32)
        inv = lax.rsqrt(jnp.mean(hidden * hidden, -1, keepdims=True) + EPS)
        normed[at.t, pl.ds(row, 16), :] = (hidden * inv * gain[...].astype(F32)).astype(BF16)

    def patch_chain(k):
        yield from scatter_x(net, at, part, 16 * k, first.at[k], second.at[k], own)
        yield from gather_x(net, at, normed, 16 * k)

    run([patch_chain(0), patch_chain(1), weights])

    def normed_cols(i):
        return normed[:, :, columns(i)].reshape(ROWS, 512)

    ready("wk", "wv", "cot", "wo")
    acc[...] = jnp.zeros_like(acc)

    @pl.loop(0, 8)
    def _(i):
        rows = normed_cols(i)
        acc[:, 0:HD] += mm(rows, wk[columns(i), :])
        acc[:, HD:2 * HD] += mm(rows, wv[columns(i), :])

    for half in range(2):
        for which in range(2):
            block = acc[half * HALF:(half + 1) * HALF, which * HD:(which + 1) * HD]
            kvb[half, at.z, at.y, at.c, which] = block.astype(BF16)
    spread = gather(net, at, kvb)
    next(spread)
    cot_chains = [gather_x(net, at, cots, 0), gather_x(net, at, cots, 16)]
    for chain in cot_chains:
        next(chain)

    acc[...] = jnp.zeros_like(acc)

    @pl.loop(0, 8)
    def _(i):
        w = jnp.concatenate([wq[half, i, y, c] for y in range(NY) for c in range(2) for half in range(2)], 0)
        acc[...] += mm(normed_cols(i), w)

    q[...] = acc[...].astype(BF16)
    q_swap = net.put(q.at[pl.ds(HALF, HALF)], qb, seq=at.twin)
    next(spread)

    def prepare(st, block, straight, turned):
        straight[st] = stack(block)
        turned[st] = straight[st].T

    prepare(0, q[0:HALF, :], qs, qt)
    top[...] = jnp.full_like(top, NEG)
    mass[...] = jnp.zeros_like(mass)
    oacc[...] = jnp.zeros_like(oacc)
    for chain in cot_chains:
        next(chain)
    offsets = next(spread)
    q_swap.wait_recv()
    prepare(1, qb[...], qs, qt)

    column = lax.broadcasted_iota(jnp.int32, (KB, GROUP * HALF), 1)
    key = lax.broadcasted_iota(jnp.int32, (KB, GROUP * HALF), 0)
    ahead[...] = (key >> 6) * ROWS + (key & (HALF - 1)) - (column & (HALF - 1))

    def keys(half, z, which):
        return kvb[half, z, :, :, which].reshape(KB, HD)

    def scores(half, z, st, masked):
        out = mm(keys(half, z, 0), qt[st]) * c2
        if masked:
            mine, other = lax.rem(at.s, 8) * ROWS, lax.rem(at.twin, 8) * ROWS + HALF
            base = mine + st * (other - mine) - half * HALF
            out = jnp.where(ahead[...] <= base, out, NEG)
        return out

    def forward(half, z, st, masked):
        out = scores(half, z, st, masked)
        old = top[st]
        new = jnp.maximum(old, jnp.max(out, 0, keepdims=True))
        fade = jnp.exp2(old - new)
        p = jnp.exp2(out - new)
        mass[st] = mass[st] * fade + jnp.sum(p, 0, keepdims=True)
        oacc[st] = oacc[st] * fade + dg(keys(half, z, 1), p.astype(BF16), TN)
        top[st] = new

    def backward(half, z, st, masked):
        prob = jnp.exp2(scores(half, z, st, masked) - lse[st])
        dprob = mm(keys(half, z, 1), gt[st])
        ds = (prob * (dprob - delta[st])).astype(BF16)
        dkv_acc[0] += mm(ds, qs[st])
        dkv_acc[1] += mm(prob.astype(BF16), gs[st])
        dqt[st] += dg(keys(half, z, 0), ds, TN)

    def tasks(body, half, z):
        @pl.loop(0, 2)
        def _(st):
            last = at.z + st * (NZ - 1 - 2 * at.z)

            @pl.when(z < last)
            def _():
                body(half, z, st, False)

            @pl.when(z == last)
            def _():
                body(half, z, st, True)

    def groups(body, offsets):
        if len(offsets) == 1:
            body(at.zz(offsets[0]))
        elif offsets:

            @pl.loop(0, 2)
            def _(k):
                body(at.zz(offsets[0] * (1 - 2 * k)))

    stage = 0
    while offsets is not None:
        groups(lambda z: tasks(forward, 1, z), offsets)
        if stage == 0:
            for chain in cot_chains:
                next(chain, None)
        if stage == 1:
            acc[...] = jnp.zeros_like(acc)

            @pl.loop(0, 8)
            def _(i):
                acc[...] += dg(cots[:, :, columns(i)].reshape(ROWS, 512), wo[:, columns(i)], NT)

            g[...] = acc[...].astype(BF16)
            g_swap = net.put(g.at[pl.ds(HALF, HALF)], gb, seq=at.twin)
        stage += 1
        offsets = next(spread, None)

    @pl.loop(0, NZ)
    def _(z):
        tasks(forward, 0, z)

    prepare(0, g[0:HALF, :], gs, gt)
    g_swap.wait_recv()
    prepare(1, gb[...], gs, gt)
    for st in range(2):
        ot = (oacc[st] / mass[st]).astype(BF16)
        lse[st] = top[st] + jnp.log2(mass[st])
        delta[st] = jnp.sum(gt[st].astype(F32) * ot.astype(F32), 0, keepdims=True)
        if st == 0:
            attn[0:HALF, :] = unstack(ot.T)
        else:
            ob[...] = unstack(ot.T)
    o_swap = net.put(ob, attn.at[pl.ds(HALF, HALF)], seq=at.twin)
    dqt[...] = jnp.zeros_like(dqt)

    def backward_group(z):
        @pl.loop(0, 2)
        def _(half):
            dkv_acc[...] = jnp.zeros_like(dkv_acc)
            tasks(backward, half, z)
            pgrad[half, z, :, :, 0] = (dkv_acc[0] * HD ** (-0.5)).astype(BF16).reshape(NY, 2, HALF, HD)
            pgrad[half, z, :, :, 1] = dkv_acc[1].astype(BF16).reshape(NY, 2, HALF, HD)

    def out(half, total):
        dkv[0, pl.ds(half * HALF, HALF), :] = total[0].astype(BF16)
        dkv[1, pl.ds(half * HALF, HALF), :] = total[1].astype(BF16)

    def layer_result(row, total):
        rows = pl.ds(row, 16)
        layer[rows, :] = (patches[rows, :].astype(F32) + total).astype(BF16)

    sums = scatter(net, at, pgrad, sib, gsum, y1, y2, za1, za2, zb1, zb2, y3, out)
    lay = []
    for stage in range(5):
        groups(backward_group, next(sums))
        if stage == 1:
            o_swap.wait_recv()

            @pl.loop(0, 8)
            def _(i):
                cols = columns(i)
                part2[:, :, cols] = mm(attn[...], wo[:, cols]).astype(BF16).reshape(NX, OWN, 512)

            lay = [
                scatter_x(net, at, part2, 16 * k, first2.at[k], second2.at[k], layer_result)
                for k in range(2)
            ]
        for chain in lay:
            next(chain, None)
    next(sums)

    attn_dq = (dqt[0] * HD ** (-0.5)).T.astype(BF16)
    dq[0:HALF, :] = unstack(attn_dq)
    dqb[...] = unstack((dqt[1] * HD ** (-0.5)).T.astype(BF16))
    dq_swap = net.put(dqb, dq.at[pl.ds(HALF, HALF)], seq=at.twin)
    next(sums)
    dq_swap.wait_recv()

    @pl.loop(0, 8)
    def _(i):
        w = jnp.concatenate([wq[half, i, y, c] for y in range(NY) for c in range(2) for half in range(2)], 0)
        grad_acc[:, columns(i)] = dg(dq[...], w, NT)

    run([sums] + lay)

    @pl.loop(0, 8)
    def _(i):
        rows = columns(i)
        total = grad_acc[:, rows] + dg(dkv[0], wk[rows, :], NT) + dg(dkv[1], wv[rows, :], NT)
        part3[:, :, rows] = total.astype(BF16).reshape(NX, OWN, 512)

    def grad_result(row, total):
        rows = pl.ds(row, 16)
        hidden = patches[rows, :].astype(F32)
        inv = lax.rsqrt(jnp.mean(hidden * hidden, -1, keepdims=True) + EPS)
        unit = hidden * inv
        scaled = total * gain[...].astype(F32)
        mean = jnp.mean(scaled * unit, -1, keepdims=True)
        cot = cots[at.t, rows, :].astype(F32)
        grad[rows, :] = (cot + inv * (scaled - unit * mean)).astype(BF16)

    run([scatter_x(net, at, part3, 16 * k, first3.at[k], second3.at[k], grad_result) for k in range(2)])
    net.finish()


def buf(*shape):
    return pltpu.VMEM(shape, BF16)


def wide(*shape):
    return pltpu.VMEM(shape, F32)


def on_device(
    byte_rows,
    patch_lengths,
    pool_query,
    pool_key,
    pool_value,
    pool_out,
    norm_gain,
    query_weight,
    key_weight,
    value_weight,
    out_weight,
    cotangent,
):
    heads = GROUP * HD
    here, there = pl.BlockSpec(memory_space=pltpu.VMEM), pl.BlockSpec(memory_space=pl.ANY)
    line = [buf(NX, OWN, D), buf(2, 2, 16, D // 2), buf(2, 2, 16, D)]
    half = (2, HALF, HD)
    scratch = [
        buf(*byte_rows.shape), buf(*pool_query.shape), buf(*pool_key.shape), buf(*pool_value.shape),
        buf(*pool_out.shape), buf(*key_weight.shape), buf(*value_weight.shape), buf(*out_weight.shape),
        buf(ROWS, 2 * HD), buf(OWN, D), buf(NX, OWN, D), buf(NX, OWN, D), buf(2, NZ, NY, 2, 32, heads),
        *line, *line, *line, wide(ROWS, D),
        wide(ROWS, heads), buf(ROWS, heads), buf(ROWS, heads), buf(HALF, heads), buf(HALF, heads),
        buf(ROWS, heads), buf(ROWS, heads), buf(HALF, heads), buf(HALF, heads),
        buf(2, NZ, NY, 2, *half), buf(2, GROUP * HALF, HD), buf(2, HD, GROUP * HALF),
        buf(2, GROUP * HALF, HD), buf(2, HD, GROUP * HALF),
        wide(2, 1, GROUP * HALF), wide(2, 1, GROUP * HALF), wide(2, HD, GROUP * HALF),
        wide(2, 1, GROUP * HALF), wide(2, 1, GROUP * HALF), wide(2, HD, GROUP * HALF), wide(2, KB, HD), pltpu.VMEM((KB, GROUP * HALF), jnp.int32),
        buf(2, NZ, NY, 2, *half), buf(2, NZ, NY, *half), buf(2, NZ, NY, *half),
        buf(NZ, *half), buf(NZ, 2, *half), buf(*half), buf(3, 2, *half),
        buf(NY, *half), buf(3, 2, NY, *half), buf(3, *half),
        buf(2, ROWS, HD),
        pltpu.SemaphoreType.DMA((288,)), pltpu.SemaphoreType.DMA((288,)), pltpu.SemaphoreType.DMA((16,)),
    ]
    rows = jax.ShapeDtypeStruct((OWN, D), BF16)
    return tuple(
        pl.pallas_call(
            kernel,
            out_shape=[rows, rows],
            in_specs=[here] * 2 + [there] * 10,
            out_specs=[here] * 2,
            scratch_shapes=scratch,
            compiler_params=pltpu.CompilerParams(
                collective_id=1, has_side_effects=True, vmem_limit_bytes=VMEM
            ),
            cost_estimate=pl.CostEstimate(flops=10**10, bytes_accessed=1 << 24, transcendentals=0),
        )(
            patch_lengths, norm_gain.reshape(1, D), byte_rows, pool_query, pool_key, pool_value, pool_out,
            query_weight, key_weight, value_weight, out_weight, cotangent,
        )
    )


def solution(mesh):
    placed = (
        P("seq", None),
        P("seq", None),
        P(None, "tensor"),
        P(None, "tensor"),
        P(None, "tensor"),
        P("tensor", None),
        P(),
        P("seq", "tensor"),
        P(None, "tensor"),
        P(None, "tensor"),
        P("tensor", None),
        P(("seq", "tensor"), None),
    )
    return jax.shard_map(
        on_device,
        mesh=mesh,
        in_specs=placed,
        out_specs=(P(("seq", "tensor"), None), P(("seq", "tensor"), None)),
        check_vma=False,
    )
```

```python
import math

import jax
import jax.numpy as jnp
from jax import lax
from jax.experimental import pallas as pl
from jax.experimental.pallas import tpu as pltpu
from jax.sharding import PartitionSpec as P

EPS = 1e-05
NEG = -1e30
MESH = pl.DeviceIdType.MESH
NZ, NY, NX = 8, 4, 4
HD = 128
GROUP = 4
ROWS = 128
HALF = 64
SHARDS = 64
D = 4096
OWN = 32
KB = 512
SENDS, RECVS = 32, 128
VMEM = 56 * 1024 * 1024
F32 = jnp.float32
BF16 = jnp.bfloat16
NT = (((1,), (1,)), ((), ()))
TN = (((0,), (0,)), ((), ()))


def mm(a, b):
    return jnp.dot(a, b, preferred_element_type=F32)


def dg(a, b, dims):
    return lax.dot_general(a, b, dims, preferred_element_type=F32)


class Place:
    def __init__(self):
        s = lax.axis_index("seq")
        self.s = s
        self.z = lax.div(s, 8)
        self.y = lax.rem(lax.div(s, 2), 4)
        self.c = lax.rem(s, 2)
        self.t = lax.axis_index("tensor")
        self.sib = self.seq(self.z, self.y, 1 - self.c)
        self.up = self.seq(self.zz(1), self.y, self.c)
        self.down = self.seq(self.zz(-1), self.y, self.c)
        self.north = self.seq(self.z, self.yy(1), self.c)
        self.south = self.seq(self.z, self.yy(-1), self.c)
        self.across = self.seq(self.z, self.yy(2), self.c)
        self.twin = SHARDS - 1 - s

    def zz(self, i):
        return lax.rem(self.z + NZ + i, NZ)

    def yy(self, i):
        return lax.rem(self.y + NY + i, NY)

    def tt(self, i):
        return lax.rem(self.t + NX + i, NX)

    def seq(self, z, y, c):
        return (z * NY + y) * 2 + c


class Net:
    def __init__(self, send, recv):
        self.send, self.recv, self.all = send, recv, []

    def put(self, src, dst, **device):
        n = len(self.all)
        if n >= SENDS:
            self.all[n - SENDS].wait_send()
        copy = pltpu.make_async_remote_copy(
            src_ref=src,
            dst_ref=dst,
            send_sem=self.send.at[n % SENDS],
            recv_sem=self.recv.at[n % RECVS],
            device_id=device,
            device_id_type=MESH,
        )
        copy.start()
        self.all.append(copy)
        return copy

    def finish(self):
        for copy in self.all[-SENDS:]:
            copy.wait_send()


def greet(devices):
    barrier = pltpu.get_barrier_semaphore()
    for device in devices:
        pl.semaphore_signal(barrier, inc=1, device_id=device, device_id_type=MESH)
    return lambda: pl.semaphore_wait(barrier, len(devices))


def partners(at):
    ring = [{"seq": d} for d in (at.sib, at.up, at.down, at.north, at.south, at.across, at.twin)]
    return ring + [{"tensor": at.tt(1)}, {"tensor": at.tt(-1)}]


def run(chains):
    chains = list(chains)
    while chains:
        left = []
        for chain in chains:
            try:
                next(chain)
                left.append(chain)
            except StopIteration:
                pass
        chains = left


def same(net, view, **device):
    return net.put(view, view, **device)


def got(copies):
    for copy in copies:
        copy.wait_recv()


def gather(net, at, buf):
    n = buf.shape[4] // 2
    zz, yy, c, y, z = at.zz, at.yy, at.c, at.y, at.z
    both, every, low, high = pl.ds(0, 2), pl.ds(0, NY), pl.ds(0, n), pl.ds(n, n)

    def z_send(i):
        up, down = buf.at[0, zz(-i), y, c], buf.at[0, zz(i), y, c]
        if i == 3:
            up, down = up.at[low], down.at[high]
        return [same(net, up, seq=at.up), same(net, down, seq=at.down)]

    def y_send(half, *offsets):
        return [
            same(net, buf.at[half, zz(o), y, c], seq=to)
            for o in offsets
            for to in (at.across, at.north, at.south)
        ]

    def group_pass(i, pairs):
        after = []
        for k in range(2):
            pair = pl.ds(2 * k, 2)
            got(pairs[k])
            go = []
            if i < 3 or k == 0:
                go.append(same(net, buf.at[1, zz(-i), pair, c], seq=at.up))
            if i < 3 or k == 1:
                go.append(same(net, buf.at[1, zz(i), pair, c], seq=at.down))
            after.append(go)
        return after

    def share(*offsets):
        return [same(net, buf.at[both, zz(o), every, c], seq=at.sib) for o in offsets]

    first = y_send(1, 0)
    zs = z_send(0)
    ys = [y_send(0, 0)]
    yield ()
    got(first)
    pairs = group_pass(0, [[], []])
    got(zs)
    zs = z_send(1)
    ys.append(y_send(0, 1, -1))
    yield ()
    got(zs)
    zs = z_send(2)
    pairs = group_pass(1, pairs)
    ys.append(y_send(0, 2, -2))
    got(ys[0])
    sib = share(0)
    yield ()
    got(zs)
    zs = z_send(3)
    pairs = group_pass(2, pairs)
    ys.append(y_send(0, 3, -3))
    got(ys[1])
    got(sib)
    sib = share(1, -1)
    yield (0,)
    got(zs)
    ys.append(y_send(0, 4))
    pairs = group_pass(3, pairs)
    got(ys[2])
    got(sib)
    sib = share(2, -2)
    yield (1, -1)
    got(ys[3])
    got(pairs[0] + pairs[1])
    got(sib)
    sib = share(3, -3)
    yield (2, -2)
    got(ys[4])
    farthest = share(4)
    got(sib)
    yield (3, -3)
    got(farthest)
    yield (4,)


def gather_x(net, at, buf, row):
    tt = at.tt
    rows, low, high = pl.ds(row, 16), pl.ds(0, D // 2), pl.ds(D // 2, D // 2)
    p = same(net, buf.at[at.t, rows], tensor=tt(1))
    m = same(net, buf.at[at.t, rows], tensor=tt(-1))
    yield
    p.wait_recv()
    m.wait_recv()
    p = same(net, buf.at[tt(-1), rows, low], tensor=tt(1))
    m = same(net, buf.at[tt(1), rows, high], tensor=tt(-1))
    yield
    p.wait_recv()
    m.wait_recv()


def add_into(ref, *others):
    total = ref[...].astype(F32)
    for other in others:
        total = total + other[...].astype(F32)
    ref[...] = total.astype(BF16)


def scatter_x(net, at, part, row, first, second, result):
    tt = at.tt
    rows, low, high = pl.ds(row, 16), pl.ds(0, D // 2), pl.ds(D // 2, D // 2)
    p = net.put(part.at[tt(2), rows, low], first.at[0], tensor=tt(1))
    m = net.put(part.at[tt(2), rows, high], first.at[1], tensor=tt(-1))
    yield
    p.wait_recv()
    add_into(part.at[tt(1), rows, low], first.at[0])
    p = net.put(part.at[tt(1), rows], second.at[0], tensor=tt(1))
    m.wait_recv()
    add_into(part.at[tt(-1), rows, high], first.at[1])
    m = net.put(part.at[tt(-1), rows], second.at[1], tensor=tt(-1))
    yield
    p.wait_recv()
    m.wait_recv()
    mine = part[at.t, rows, :].astype(F32)
    result(row, mine + second[0].astype(F32) + second[1].astype(F32))


def slot(o):
    return o % NZ


def scatter(net, at, part, sib, acc, y_next, za_first, za_next, zb_first, zb_next, y_last, out):
    zz, yy = at.zz, at.yy
    both, every = pl.ds(0, 2), pl.ds(0, NY)
    one, two = pl.ds(0, 1), pl.ds(1, 1)
    low, high = pl.ds(0, 2), pl.ds(2, 2)
    ways = ((2, at.across), (1, at.north), (-1, at.south))
    near, ys, ring0, ring1 = {}, {}, {}, {}

    def share(offsets):
        for o in offsets:
            near[o] = net.put(part.at[both, zz(o), every, 1 - at.c], sib.at[both, zz(o)], seq=at.sib)

    def own(offsets):
        for o in offsets:
            near[o].wait_recv()
            z = zz(o)
            acc[:, z] = (part[:, z, :, at.c].astype(F32) + sib[:, z].astype(F32)).astype(BF16)

    def y_send(offsets):
        for o in offsets:
            ys[o] = [
                net.put(acc.at[0, zz(o), yy(j)], y_next.at[slot(o), k], seq=to)
                for k, (j, to) in enumerate(ways)
            ]

    def y_sum(o, *came):
        got(ys[o])
        total = acc[0, zz(o), at.y].astype(F32)
        for k in range(3):
            total = total + y_next[slot(o), k].astype(F32)
        for ref in came:
            total = total + ref[...].astype(F32)
        return total

    def z_zero(i):
        if i < 4:
            got(ring0[i + 1])
        if i == 0:
            out(0, y_sum(0, za_next.at[0, 0], za_next.at[0, 1]))
            return
        for side, o in enumerate((i, -i)[:1 if i == 4 else 2]):
            came = [za_next.at[i, side]] if i < 3 else []
            acc[0, zz(o), at.y] = y_sum(o, *came).astype(BF16)
        if i == 3:
            add_into(acc.at[0, zz(3), at.y, one], za_first.at[one])
            add_into(acc.at[0, zz(-3), at.y, two], za_first.at[two])
        if i == 4:
            src = acc.at[0, zz(4), at.y]
            ring0[4] = [
                net.put(src.at[one], za_first.at[one], seq=at.up),
                net.put(src.at[two], za_first.at[two], seq=at.down),
            ]
            return
        ring0[i] = [
            net.put(acc.at[0, zz(i), at.y], za_next.at[i - 1, 0], seq=at.up),
            net.put(acc.at[0, zz(-i), at.y], za_next.at[i - 1, 1], seq=at.down),
        ]

    def z_one(i):
        if i == 4:
            ring1[4] = [
                net.put(acc.at[1, zz(4), low], zb_first.at[low], seq=at.up),
                net.put(acc.at[1, zz(4), high], zb_first.at[high], seq=at.down),
            ]
            return
        if i == 3:
            got(ring1[4])
            add_into(acc.at[1, zz(3), low], zb_first.at[low])
            add_into(acc.at[1, zz(-3), high], zb_first.at[high])
        go = []
        for k, pair in enumerate((low, high)):
            for side, o, to in ((0, i, at.up), (1, -i, at.down)):
                if i < 3:
                    ring1[i + 1][2 * k + side].wait_recv()
                    add_into(acc.at[1, zz(o), pair], zb_next.at[i, side, pair])
                go.append(net.put(acc.at[1, zz(o), pair], zb_next.at[i - 1, side, pair], seq=to))
        ring1[i] = go

    rounds = ((4,), (3, -3), (2, -2), (1, -1), (0,))
    yield rounds[0]
    share(rounds[0])
    for r in range(1, 5):
        yield rounds[r]
        share(rounds[r])
        own(rounds[r - 1])
        z_one(5 - r)
        y_send(rounds[r - 1])
        if r > 1:
            z_zero(6 - r)
    yield ()
    own(rounds[4])
    y_send(rounds[4])
    got(ring1[1])
    add_into(acc.at[1, at.z], zb_next.at[0, 0], zb_next.at[0, 1])
    last = [net.put(acc.at[1, at.z, yy(j)], y_last.at[k], seq=to) for k, (j, to) in enumerate(ways)]
    z_zero(1)
    yield ()
    got(last)
    block = acc[1, at.z, at.y].astype(F32)
    for k in range(3):
        block = block + y_last[k].astype(F32)
    out(1, block)
    z_zero(0)


def pool(lengths, byte, pool_query, pool_key, pool_value):
    nb = byte.shape[0]
    count = lengths[...].astype(F32)
    row = lax.broadcasted_iota(jnp.int32, (ROWS, ROWS), 0)
    col = lax.broadcasted_iota(jnp.int32, (ROWS, ROWS), 1)
    ends = jnp.sum(jnp.where(col <= row, count, 0.0), 1, keepdims=True)
    size = jnp.sum(jnp.where(col == row, count, 0.0), 1, keepdims=True)
    where_at = lax.broadcasted_iota(jnp.int32, (ROWS, nb), 1).astype(F32)
    member = (where_at >= ends - size) & (where_at < ends)
    sums = mm(jnp.where(member, 1.0, 0.0).astype(BF16), byte[...])
    means = (sums / size).astype(BF16)
    pq = mm(means, pool_query[...]).astype(BF16)
    pk = mm(byte[...], pool_key[...]).astype(BF16)
    pv = mm(byte[...], pool_value[...]).astype(BF16)
    heads = []
    for h in range(pq.shape[1] // HD):
        cols = slice(h * HD, (h + 1) * HD)
        scores = jnp.where(member, dg(pq[:, cols], pk[:, cols], NT) * HD ** (-0.5), NEG)
        expo = jnp.exp(scores - jnp.max(scores, -1, keepdims=True))
        weights = (expo / jnp.sum(expo, -1, keepdims=True)).astype(BF16)
        heads.append(mm(weights, pv[:, cols]))
    return jnp.concatenate(heads, 1).astype(BF16)


def stack(block):
    return jnp.concatenate([block[:, h * HD:(h + 1) * HD] for h in range(GROUP)], 0)


def unstack(value):
    return jnp.concatenate([value[h * HALF:(h + 1) * HALF] for h in range(GROUP)], 1)


def columns(i):
    return pl.ds(pl.multiple_of(i * 512, 512), 512)


def kernel(
    lengths, gain, byte_h, pq_h, pk_h, pv_h, po_h, wq_h, wk_h, wv_h, wo_h, cot_h,
    layer, grad,
    byte, pool_q, pool_k, pool_v, pool_o, wkv, wo, pooled, patches, normed, cots, wq,
    part, first, second, part2, first2, second2, part3, first3, second3, grad_acc,
    acc, q, g, qb, gb, attn, dq, ob, dqb,
    kvb, qs, qt, gs, gt, top, mass, oacc, lse, delta, dqt, dkv_acc, ahead,
    pgrad, sib, gsum, y1, za1, za2, zb1, zb2, y2, dkv,
    send, recv, local,
):
    at = Place()
    net = Net(send, recv)
    c2 = HD ** (-0.5) * math.log2(math.e)
    loads = {}

    def load(name, src, dst):
        copy = pltpu.make_async_copy(src, dst, local.at[len(loads)])
        copy.start()
        loads[name] = copy

    def ready(*names):
        for name in names:
            loads[name].wait()

    for half in range(2):
        load("wq%d" % half, wq_h.at[pl.ds(half * 32, 32)], wq.at[half, at.z, at.y, at.c])
    load("byte", byte_h, byte)
    load("pq", pq_h, pool_q)
    load("pk", pk_h, pool_k)
    load("pv", pv_h, pool_v)
    load("po", po_h, pool_o)
    load("cot", cot_h, cots.at[at.t])
    load("wk", wk_h, wkv.at[:, pl.ds(0, HD)])
    load("wv", wv_h, wkv.at[:, pl.ds(HD, HD)])
    load("wo", wo_h, wo)
    all_here = greet(partners(at))

    ready("byte", "pq", "pk", "pv")
    pooled[...] = pool(lengths, byte, pool_q, pool_k, pool_v)
    ready("po")
    for i in range(8):
        cols = pl.ds(i * 512, 512)
        part[:, :, cols] = mm(pooled[...], pool_o[:, cols]).astype(BF16).reshape(NX, OWN, 512)
    ready("wq0", "wq1")
    all_here()

    def own(row, total):
        rows = total.astype(BF16)
        patches[pl.ds(row, 16), :] = rows
        hidden = rows.astype(F32)
        inv = lax.rsqrt(jnp.mean(hidden * hidden, -1, keepdims=True) + EPS)
        normed[at.t, pl.ds(row, 16), :] = (hidden * inv * gain[...].reshape(1, D).astype(F32)).astype(BF16)

    def patch_chain(k):
        yield from scatter_x(net, at, part, 16 * k, first.at[k], second.at[k], own)
        yield from gather_x(net, at, normed, 16 * k)

    chains = [patch_chain(0), patch_chain(1)]
    for chain in chains:
        next(chain)
    weights = gather(net, at, wq)
    next(weights)
    for turn in range(4):
        for chain in chains:
            next(chain, None)
        if turn < 3:
            next(weights)

    def normed_cols(i):
        return normed[:, :, columns(i)].reshape(ROWS, 512)

    ready("wk", "wv", "cot", "wo")
    acc[:, 0:2 * HD] = jnp.zeros((ROWS, 2 * HD), F32)

    @pl.loop(0, 8)
    def _(i):
        acc[:, 0:2 * HD] += mm(normed_cols(i), wkv[columns(i), :])

    for half in range(2):
        for which in range(2):
            block = acc[half * HALF:(half + 1) * HALF, which * HD:(which + 1) * HD]
            kvb[half, at.z, at.y, at.c, which] = block.astype(BF16)
    spread = gather(net, at, kvb)
    next(spread)
    cot_chains = [gather_x(net, at, cots, 0), gather_x(net, at, cots, 16)]
    for chain in cot_chains:
        next(chain)
    next(weights)
    next(weights)
    next(spread)
    run([weights])
    acc[...] = jnp.zeros_like(acc)

    @pl.loop(0, 8)
    def _(i):
        w = jnp.concatenate([wq[half, i, y, c] for y in range(NY) for c in range(2) for half in range(2)], 0)
        acc[...] += mm(normed_cols(i), w)

    q[...] = acc[...].astype(BF16)
    q_swap = net.put(q.at[pl.ds(HALF, HALF)], qb, seq=at.twin)
    for chain in cot_chains:
        next(chain)
    next(spread)

    def prepare(st, block, straight, turned):
        straight[st] = stack(block)
        turned[st] = straight[st].T

    prepare(0, q[0:HALF, :], qs, qt)
    top[...] = jnp.full_like(top, NEG)
    mass[...] = jnp.zeros_like(mass)
    oacc[...] = jnp.zeros_like(oacc)
    run(cot_chains)
    acc[...] = jnp.zeros_like(acc)

    @pl.loop(0, 8)
    def _(i):
        acc[...] += dg(cots[:, :, columns(i)].reshape(ROWS, 512), wo[:, columns(i)], NT)

    g[...] = acc[...].astype(BF16)
    g_swap = net.put(g.at[pl.ds(HALF, HALF)], gb, seq=at.twin)
    offsets = next(spread)
    q_swap.wait_recv()
    prepare(1, qb[...], qs, qt)

    column = lax.broadcasted_iota(jnp.int32, (KB, GROUP * HALF), 1)
    key = lax.broadcasted_iota(jnp.int32, (KB, GROUP * HALF), 0)
    ahead[...] = (key >> 6) * ROWS + (key & (HALF - 1)) - (column & (HALF - 1))

    def keys(half, z, which):
        return kvb[half, z, :, :, which].reshape(KB, HD)

    def scores(half, z, st, masked):
        out = mm(keys(half, z, 0), qt[st]) * c2
        if masked:
            mine, other = lax.rem(at.s, 8) * ROWS, lax.rem(at.twin, 8) * ROWS + HALF
            base = mine + st * (other - mine) - half * HALF
            out = jnp.where(ahead[...] <= base, out, NEG)
        return out

    def forward(half, z, st, masked):
        out = scores(half, z, st, masked)
        old = top[st]
        new = jnp.maximum(old, jnp.max(out, 0, keepdims=True))
        fade = jnp.exp2(old - new)
        p = jnp.exp2(out - new)
        mass[st] = mass[st] * fade + jnp.sum(p, 0, keepdims=True)
        oacc[st] = oacc[st] * fade + dg(keys(half, z, 1), p.astype(BF16), TN)
        top[st] = new

    def backward(half, z, st, masked):
        prob = jnp.exp2(scores(half, z, st, masked) - lse[st])
        dprob = mm(keys(half, z, 1), gt[st])
        ds = (prob * (dprob - delta[st])).astype(BF16)
        dkv_acc[0] += mm(ds, qs[st])
        dkv_acc[1] += mm(prob.astype(BF16), gs[st])
        dqt[st] += dg(keys(half, z, 0), ds, TN)

    def tasks(body, half, z):
        @pl.loop(0, 2)
        def _(st):
            last = at.z + st * (NZ - 1 - 2 * at.z)

            @pl.when(z < last)
            def _():
                body(half, z, st, False)

            @pl.when(z == last)
            def _():
                body(half, z, st, True)

    def groups(body, offsets):
        if len(offsets) == 1:
            body(at.zz(offsets[0]))
        elif offsets:

            @pl.loop(0, 2)
            def _(k):
                body(at.zz(offsets[0] * (1 - 2 * k)))

    def forward_group(z):
        @pl.loop(0, 2)
        def _(half):
            tasks(forward, half, z)

    while offsets is not None:
        groups(forward_group, offsets)
        offsets = next(spread, None)

    prepare(0, g[0:HALF, :], gs, gt)
    g_swap.wait_recv()
    prepare(1, gb[...], gs, gt)
    for st in range(2):
        ot = (oacc[st] / mass[st]).astype(BF16)
        lse[st] = top[st] + jnp.log2(mass[st])
        delta[st] = jnp.sum(gt[st].astype(F32) * ot.astype(F32), 0, keepdims=True)
        if st == 0:
            attn[0:HALF, :] = unstack(ot.T)
        else:
            ob[...] = unstack(ot.T)
    o_swap = net.put(ob, attn.at[pl.ds(HALF, HALF)], seq=at.twin)
    dqt[...] = jnp.zeros_like(dqt)

    def backward_group(z):
        @pl.loop(0, 2)
        def _(half):
            dkv_acc[...] = jnp.zeros_like(dkv_acc)
            tasks(backward, half, z)
            pgrad[half, z, :, :, 0] = (dkv_acc[0] * HD ** (-0.5)).astype(BF16).reshape(NY, 2, HALF, HD)
            pgrad[half, z, :, :, 1] = dkv_acc[1].astype(BF16).reshape(NY, 2, HALF, HD)

    def out(half, total):
        dkv[half * HALF:(half + 1) * HALF, 0:HD] = total[0].astype(BF16)
        dkv[half * HALF:(half + 1) * HALF, HD:2 * HD] = total[1].astype(BF16)

    def layer_result(row, total):
        rows = pl.ds(row, 16)
        layer[rows, :] = (patches[rows, :].astype(F32) + total).astype(BF16)

    sums = scatter(net, at, pgrad, sib, gsum, y1, za1, za2, zb1, zb2, y2, out)
    for stage in range(5):
        groups(backward_group, next(sums))
        if stage == 2:
            o_swap.wait_recv()

            @pl.loop(0, 8)
            def _(i):
                cols = columns(i)
                part2[:, :, cols] = mm(attn[...], wo[:, cols]).astype(BF16).reshape(NX, OWN, 512)

            lay = [
                scatter_x(net, at, part2, 16 * k, first2.at[k], second2.at[k], layer_result)
                for k in range(2)
            ]
        if stage == 2 or stage == 4:
            for chain in lay:
                next(chain)
    next(sums)

    dq[0:HALF, :] = unstack((dqt[0] * HD ** (-0.5)).T.astype(BF16))
    dqb[...] = unstack((dqt[1] * HD ** (-0.5)).T.astype(BF16))
    dq_swap = net.put(dqb, dq.at[pl.ds(HALF, HALF)], seq=at.twin)
    next(sums)
    dq_swap.wait_recv()

    @pl.loop(0, 8)
    def _(i):
        w = jnp.concatenate([wq[half, i, y, c] for y in range(NY) for c in range(2) for half in range(2)], 0)
        grad_acc[:, columns(i)] = dg(dq[...], w, NT)

    run([sums])

    @pl.loop(0, 8)
    def _(i):
        rows = columns(i)
        total = grad_acc[:, rows] + dg(dkv[...], wkv[rows, :], NT)
        part3[:, :, rows] = total.astype(BF16).reshape(NX, OWN, 512)

    def grad_result(row, total):
        rows = pl.ds(row, 16)
        hidden = patches[rows, :].astype(F32)
        inv = lax.rsqrt(jnp.mean(hidden * hidden, -1, keepdims=True) + EPS)
        unit = hidden * inv
        scaled = total * gain[...].reshape(1, D).astype(F32)
        mean = jnp.mean(scaled * unit, -1, keepdims=True)
        cot = cots[at.t, rows, :].astype(F32)
        grad[rows, :] = (cot + inv * (scaled - unit * mean)).astype(BF16)

    run([scatter_x(net, at, part3, 16 * k, first3.at[k], second3.at[k], grad_result) for k in range(2)] + lay)
    net.finish()


def buf(*shape):
    return pltpu.VMEM(shape, BF16)


def wide(*shape):
    return pltpu.VMEM(shape, F32)


def finish_kernel(layer, grad, layer_out, patch_grad):
    layer_out[...] = layer[...]
    patch_grad[...] = grad[...]


def finish(layer, grad):
    here = pl.BlockSpec(memory_space=pltpu.VMEM)
    rows = jax.ShapeDtypeStruct((OWN, D), BF16)
    return tuple(
        pl.pallas_call(finish_kernel, out_shape=[rows, rows], in_specs=[here] * 2, out_specs=[here] * 2)(
            layer, grad
        )
    )


def on_device(
    byte_rows,
    patch_lengths,
    pool_query,
    pool_key,
    pool_value,
    pool_out,
    norm_gain,
    query_weight,
    key_weight,
    value_weight,
    out_weight,
    cotangent,
):
    heads = GROUP * HD
    here, there = pl.BlockSpec(memory_space=pltpu.VMEM), pl.BlockSpec(memory_space=pl.ANY)
    line = [buf(NX, OWN, D), buf(2, 2, 16, D // 2), buf(2, 2, 16, D)]
    half = (2, HALF, HD)
    scratch = [
        buf(*byte_rows.shape), buf(*pool_query.shape), buf(*pool_key.shape), buf(*pool_value.shape),
        buf(*pool_out.shape), buf(D, 2 * HD), buf(*out_weight.shape),
        buf(ROWS, 2 * HD), buf(OWN, D), buf(NX, OWN, D), buf(NX, OWN, D), buf(2, NZ, NY, 2, 32, heads),
        *line, *line, *line, wide(ROWS, D),
        wide(ROWS, heads), buf(ROWS, heads), buf(ROWS, heads), buf(HALF, heads), buf(HALF, heads),
        buf(ROWS, heads), buf(ROWS, heads), buf(HALF, heads), buf(HALF, heads),
        buf(2, NZ, NY, 2, *half), buf(2, GROUP * HALF, HD), buf(2, HD, GROUP * HALF),
        buf(2, GROUP * HALF, HD), buf(2, HD, GROUP * HALF),
        wide(2, 1, GROUP * HALF), wide(2, 1, GROUP * HALF), wide(2, HD, GROUP * HALF),
        wide(2, 1, GROUP * HALF), wide(2, 1, GROUP * HALF), wide(2, HD, GROUP * HALF), wide(2, KB, HD), pltpu.VMEM((KB, GROUP * HALF), jnp.int32),
        buf(2, NZ, NY, 2, *half), buf(2, NZ, NY, *half), buf(2, NZ, NY, *half),
        buf(NZ, 3, *half), buf(*half), buf(3, 2, *half),
        buf(NY, *half), buf(3, 2, NY, *half), buf(3, *half),
        buf(ROWS, 2 * HD),
        pltpu.SemaphoreType.DMA((SENDS,)), pltpu.SemaphoreType.DMA((RECVS,)), pltpu.SemaphoreType.DMA((16,)),
    ]
    rows = jax.ShapeDtypeStruct((OWN, D), BF16)
    return finish(
        *pl.pallas_call(
            kernel,
            out_shape=[rows, rows],
            in_specs=[here] * 2 + [there] * 10,
            out_specs=[here] * 2,
            scratch_shapes=scratch,
            compiler_params=pltpu.CompilerParams(
                collective_id=1, has_side_effects=True, vmem_limit_bytes=VMEM
            ),
            cost_estimate=pl.CostEstimate(flops=10**10, bytes_accessed=1 << 24, transcendentals=0),
        )(
            patch_lengths, norm_gain, byte_rows, pool_query, pool_key, pool_value, pool_out,
            query_weight, key_weight, value_weight, out_weight, cotangent,
        )
    )


def solution(mesh):
    placed = (
        P("seq", None),
        P("seq", None),
        P(None, "tensor"),
        P(None, "tensor"),
        P(None, "tensor"),
        P("tensor", None),
        P(),
        P("seq", "tensor"),
        P(None, "tensor"),
        P(None, "tensor"),
        P("tensor", None),
        P(("seq", "tensor"), None),
    )
    return jax.shard_map(
        on_device,
        mesh=mesh,
        in_specs=placed,
        out_specs=(P(("seq", "tensor"), None), P(("seq", "tensor"), None)),
        check_vma=False,
    )
```

```python
import math

import jax
import jax.numpy as jnp
from jax import lax
from jax.experimental import pallas as pl
from jax.experimental.pallas import tpu as pltpu
from jax.sharding import PartitionSpec as P

EPS = 1e-05
NEG = -1e30
MESH = pl.DeviceIdType.MESH
NZ, NY, NX = 8, 4, 4
HD = 128
GROUP = 4
ROWS = 128
HALF = 64
SHARDS = 64
D = 4096
OWN = 32
KB = 512
SENDS, RECVS = 32, 128
VMEM = 56 * 1024 * 1024
F32 = jnp.float32
BF16 = jnp.bfloat16
NT = (((1,), (1,)), ((), ()))
TN = (((0,), (0,)), ((), ()))


def mm(a, b):
    return jnp.dot(a, b, preferred_element_type=F32)


def dg(a, b, dims):
    return lax.dot_general(a, b, dims, preferred_element_type=F32)


class Place:
    def __init__(self):
        s = lax.axis_index("seq")
        self.s = s
        self.z = lax.div(s, 8)
        self.y = lax.rem(lax.div(s, 2), 4)
        self.c = lax.rem(s, 2)
        self.t = lax.axis_index("tensor")
        self.sib = self.seq(self.z, self.y, 1 - self.c)
        self.up, self.down = self.along(1), self.along(-1)
        self.north = self.seq(self.z, self.yy(1), self.c)
        self.south = self.seq(self.z, self.yy(-1), self.c)
        self.across = self.seq(self.z, self.yy(2), self.c)

    def along(self, i):
        return self.seq(self.zz(i), self.y, self.c)

    def zz(self, i):
        return lax.rem(self.z + NZ + i, NZ)

    def yy(self, i):
        return lax.rem(self.y + NY + i, NY)

    def tt(self, i):
        return lax.rem(self.t + NX + i, NX)

    def seq(self, z, y, c):
        return (z * NY + y) * 2 + c


class Net:
    def __init__(self, send, recv):
        self.send, self.recv, self.all = send, recv, []

    def put(self, src, dst, **device):
        n = len(self.all)
        if n >= SENDS:
            self.all[n - SENDS].wait_send()
        copy = pltpu.make_async_remote_copy(
            src_ref=src,
            dst_ref=dst,
            send_sem=self.send.at[n % SENDS],
            recv_sem=self.recv.at[n % RECVS],
            device_id=device,
            device_id_type=MESH,
        )
        copy.start()
        self.all.append(copy)
        return copy

    def finish(self):
        for copy in self.all[-SENDS:]:
            copy.wait_send()


def greet(devices):
    barrier = pltpu.get_barrier_semaphore()
    for device in devices:
        pl.semaphore_signal(barrier, inc=1, device_id=device, device_id_type=MESH)
    return lambda: pl.semaphore_wait(barrier, len(devices))


def partners(at):
    ring = [{"seq": d} for d in (at.sib, at.up, at.down, at.north, at.south, at.across)]
    ring += [{"seq": at.along(i)} for i in (2, -2, 3, -3, 4)]
    return ring + [{"tensor": at.tt(1)}, {"tensor": at.tt(-1)}]


def run(chains):
    chains = list(chains)
    while chains:
        left = []
        for chain in chains:
            try:
                next(chain)
                left.append(chain)
            except StopIteration:
                pass
        chains = left


def same(net, view, **device):
    return net.put(view, view, **device)


def got(copies):
    for copy in copies:
        copy.wait_recv()


def gather(net, at, buf):
    n = buf.shape[4] // 2
    zz, yy, c, y, z = at.zz, at.yy, at.c, at.y, at.z
    both, every, low, high = pl.ds(0, 2), pl.ds(0, NY), pl.ds(0, n), pl.ds(n, n)

    def z_send(i):
        up, down = buf.at[0, zz(-i), y, c], buf.at[0, zz(i), y, c]
        if i == 3:
            up, down = up.at[low], down.at[high]
        return [same(net, up, seq=at.up), same(net, down, seq=at.down)]

    def y_send(half, *offsets):
        return [
            same(net, buf.at[half, zz(o), y, c], seq=to)
            for o in offsets
            for to in (at.across, at.north, at.south)
        ]

    def group_pass(i, pairs):
        after = []
        for k in range(2):
            pair = pl.ds(2 * k, 2)
            got(pairs[k])
            go = []
            if i < 3 or k == 0:
                go.append(same(net, buf.at[1, zz(-i), pair, c], seq=at.up))
            if i < 3 or k == 1:
                go.append(same(net, buf.at[1, zz(i), pair, c], seq=at.down))
            after.append(go)
        return after

    def share(*offsets):
        return [same(net, buf.at[both, zz(o), every, c], seq=at.sib) for o in offsets]

    first = y_send(1, 0)
    zs = z_send(0)
    ys = [y_send(0, 0)]
    yield ()
    got(first)
    pairs = group_pass(0, [[], []])
    got(zs)
    zs = z_send(1)
    ys.append(y_send(0, 1, -1))
    yield ()
    pairs = group_pass(1, pairs)
    got(zs)
    zs = z_send(2)
    got(ys[0])
    sib = share(0)
    ys.append(y_send(0, 2, -2))
    yield ()
    pairs = group_pass(2, pairs)
    got(zs)
    zs = z_send(3)
    got(ys[1])
    last, sib = sib, share(1, -1)
    ys.append(y_send(0, 3, -3))
    got(last)
    yield (0,)
    pairs = group_pass(3, pairs)
    got(zs)
    ys.append(y_send(0, 4))
    got(ys[2])
    last, sib = sib, share(2, -2)
    got(last)
    yield (1, -1)
    got(pairs[0] + pairs[1])
    got(ys[3])
    last, sib = sib, share(3, -3)
    got(last)
    yield (2, -2)
    got(ys[4])
    last, sib = sib, share(4)
    got(last)
    yield (3, -3)
    got(sib)
    yield (4,)


def gather_far(net, at, buf):
    zz, yy, c, y, z = at.zz, at.yy, at.c, at.y, at.z
    every, all_z = pl.ds(0, NY), pl.ds(0, NZ)
    y_ways = (at.across, at.north, at.south)

    def step(i, pairs):
        after = []
        for k in range(2):
            pair = pl.ds(2 * k, 2)
            got(pairs[k])
            go = []
            if i < 3 or k == 0:
                go.append(same(net, buf.at[1, zz(-i), pair, c], seq=at.up))
            if i < 3 or k == 1:
                go.append(same(net, buf.at[1, zz(i), pair, c], seq=at.down))
            after.append(go)
        return after

    def share(*offsets):
        return [same(net, buf.at[1, zz(o), every, c], seq=at.sib) for o in offsets]

    first = [same(net, buf.at[1, z, y, c], seq=to) for to in y_ways]
    zs = [same(net, buf.at[0, z, y, c], seq=at.along(i)) for i in (1, -1, 2, -2, 3, -3, 4)]
    yield
    got(first)
    pairs = step(0, [[], []])
    got(zs)
    ys = [same(net, buf.at[0, all_z, y, c], seq=to) for to in y_ways]
    sib = share(0)
    yield
    pairs = step(1, pairs)
    sib += share(1, -1)
    yield
    pairs = step(2, pairs)
    sib += share(2, -2)
    yield
    pairs = step(3, pairs)
    sib += share(3, -3)
    got(ys)
    sib += [same(net, buf.at[0, all_z, yy(j), c], seq=at.sib) for j in range(4)]
    yield
    got(pairs[0] + pairs[1])
    sib += share(4)
    yield
    got(sib)


def gather_x(net, at, buf, row):
    tt = at.tt
    rows, low, high = pl.ds(row, 16), pl.ds(0, D // 2), pl.ds(D // 2, D // 2)
    p = same(net, buf.at[at.t, rows], tensor=tt(1))
    m = same(net, buf.at[at.t, rows], tensor=tt(-1))
    yield
    p.wait_recv()
    m.wait_recv()
    p = same(net, buf.at[tt(-1), rows, low], tensor=tt(1))
    m = same(net, buf.at[tt(1), rows, high], tensor=tt(-1))
    yield
    p.wait_recv()
    m.wait_recv()


def add_into(ref, *others):
    total = ref[...].astype(F32)
    for other in others:
        total = total + other[...].astype(F32)
    ref[...] = total.astype(BF16)


def scatter_x(net, at, part, row, first, second, result):
    tt = at.tt
    rows, low, high = pl.ds(row, 16), pl.ds(0, D // 2), pl.ds(D // 2, D // 2)
    p = net.put(part.at[tt(2), rows, low], first.at[0], tensor=tt(1))
    m = net.put(part.at[tt(2), rows, high], first.at[1], tensor=tt(-1))
    yield
    p.wait_recv()
    add_into(part.at[tt(1), rows, low], first.at[0])
    p = net.put(part.at[tt(1), rows], second.at[0], tensor=tt(1))
    m.wait_recv()
    add_into(part.at[tt(-1), rows, high], first.at[1])
    m = net.put(part.at[tt(-1), rows], second.at[1], tensor=tt(-1))
    yield
    p.wait_recv()
    m.wait_recv()
    mine = part[at.t, rows, :].astype(F32)
    result(row, mine + second[0].astype(F32) + second[1].astype(F32))


def slot(o):
    return o % NZ


def scatter(net, at, part, sib, acc, y_next, za_first, za_next, zb_first, zb_next, y_last, out):
    zz, yy = at.zz, at.yy
    both, every = pl.ds(0, 2), pl.ds(0, NY)
    one, two = pl.ds(0, 1), pl.ds(1, 1)
    low, high = pl.ds(0, 2), pl.ds(2, 2)
    ways = ((2, at.across), (1, at.north), (-1, at.south))
    near, ys, ring0, ring1 = {}, {}, {}, {}

    def share(offsets):
        for o in offsets:
            near[o] = net.put(part.at[both, zz(o), every, 1 - at.c], sib.at[both, zz(o)], seq=at.sib)

    def own(offsets):
        for o in offsets:
            near[o].wait_recv()
            z = zz(o)
            acc[:, z] = (part[:, z, :, at.c].astype(F32) + sib[:, z].astype(F32)).astype(BF16)

    def y_send(offsets):
        for o in offsets:
            ys[o] = [
                net.put(acc.at[0, zz(o), yy(j)], y_next.at[slot(o), k], seq=to)
                for k, (j, to) in enumerate(ways)
            ]

    def y_sum(o, *came):
        got(ys[o])
        total = acc[0, zz(o), at.y].astype(F32)
        for k in range(3):
            total = total + y_next[slot(o), k].astype(F32)
        for ref in came:
            total = total + ref[...].astype(F32)
        return total

    def z_zero(i):
        if i < 4:
            got(ring0[i + 1])
        if i == 0:
            out(0, y_sum(0, za_next.at[0, 0], za_next.at[0, 1]))
            return
        for side, o in enumerate((i, -i)[:1 if i == 4 else 2]):
            came = [za_next.at[i, side]] if i < 3 else []
            acc[0, zz(o), at.y] = y_sum(o, *came).astype(BF16)
        if i == 3:
            add_into(acc.at[0, zz(3), at.y, one], za_first.at[one])
            add_into(acc.at[0, zz(-3), at.y, two], za_first.at[two])
        if i == 4:
            src = acc.at[0, zz(4), at.y]
            ring0[4] = [
                net.put(src.at[one], za_first.at[one], seq=at.up),
                net.put(src.at[two], za_first.at[two], seq=at.down),
            ]
            return
        ring0[i] = [
            net.put(acc.at[0, zz(i), at.y], za_next.at[i - 1, 0], seq=at.up),
            net.put(acc.at[0, zz(-i), at.y], za_next.at[i - 1, 1], seq=at.down),
        ]

    def z_one(i):
        if i == 4:
            ring1[4] = [
                net.put(acc.at[1, zz(4), low], zb_first.at[low], seq=at.up),
                net.put(acc.at[1, zz(4), high], zb_first.at[high], seq=at.down),
            ]
            return
        if i == 3:
            got(ring1[4])
            add_into(acc.at[1, zz(3), low], zb_first.at[low])
            add_into(acc.at[1, zz(-3), high], zb_first.at[high])
        go = []
        for k, pair in enumerate((low, high)):
            for side, o, to in ((0, i, at.up), (1, -i, at.down)):
                if i < 3:
                    ring1[i + 1][2 * k + side].wait_recv()
                    add_into(acc.at[1, zz(o), pair], zb_next.at[i, side, pair])
                go.append(net.put(acc.at[1, zz(o), pair], zb_next.at[i - 1, side, pair], seq=to))
        ring1[i] = go

    rounds = ((4,), (3, -3), (2, -2), (1, -1), (0,))
    yield rounds[0]
    share(rounds[0])
    for r in range(1, 5):
        yield rounds[r]
        share(rounds[r])
        own(rounds[r - 1])
        z_one(5 - r)
        y_send(rounds[r - 1])
        if r > 1:
            z_zero(6 - r)
    yield ()
    own(rounds[4])
    y_send(rounds[4])
    got(ring1[1])
    add_into(acc.at[1, at.z], zb_next.at[0, 0], zb_next.at[0, 1])
    last = [net.put(acc.at[1, at.z, yy(j)], y_last.at[k], seq=to) for k, (j, to) in enumerate(ways)]
    z_zero(1)
    yield ()
    got(last)
    block = acc[1, at.z, at.y].astype(F32)
    for k in range(3):
        block = block + y_last[k].astype(F32)
    out(1, block)
    z_zero(0)


def pool(lengths, byte, pool_query, pool_key, pool_value):
    nb = byte.shape[0]
    count = lengths[...].astype(F32)
    row = lax.broadcasted_iota(jnp.int32, (ROWS, ROWS), 0)
    col = lax.broadcasted_iota(jnp.int32, (ROWS, ROWS), 1)
    ends = jnp.sum(jnp.where(col <= row, count, 0.0), 1, keepdims=True)
    size = jnp.sum(jnp.where(col == row, count, 0.0), 1, keepdims=True)
    where_at = lax.broadcasted_iota(jnp.int32, (ROWS, nb), 1).astype(F32)
    member = (where_at >= ends - size) & (where_at < ends)
    sums = mm(jnp.where(member, 1.0, 0.0).astype(BF16), byte[...])
    means = (sums / size).astype(BF16)
    pq = mm(means, pool_query[...]).astype(BF16)
    pk = mm(byte[...], pool_key[...]).astype(BF16)
    pv = mm(byte[...], pool_value[...]).astype(BF16)
    heads = []
    for h in range(pq.shape[1] // HD):
        cols = slice(h * HD, (h + 1) * HD)
        scores = jnp.where(member, dg(pq[:, cols], pk[:, cols], NT) * HD ** (-0.5), NEG)
        expo = jnp.exp(scores - jnp.max(scores, -1, keepdims=True))
        weights = (expo / jnp.sum(expo, -1, keepdims=True)).astype(BF16)
        heads.append(mm(weights, pv[:, cols]))
    return jnp.concatenate(heads, 1).astype(BF16)


def stack(block):
    return jnp.concatenate([block[:, h * HD:(h + 1) * HD] for h in range(GROUP)], 0)


def unstack(value):
    return jnp.concatenate([value[h * ROWS:(h + 1) * ROWS] for h in range(GROUP)], 1)


def columns(i):
    return pl.ds(pl.multiple_of(i * 512, 512), 512)


def kernel(
    lengths, gain, byte_h, pq_h, pk_h, pv_h, po_h, wq_h, wk_h, wv_h, wo_h, cot_h,
    layer, grad,
    byte, pool_q, pool_k, pool_v, pool_o, wkv, wo, pooled, patches, normed, cots, wq,
    part, first, second, part2, first2, second2, part3, first3, second3, grad_acc,
    acc, attn, dq,
    kvb, qs, qt, gs, gt, top, mass, oacc, lse, delta, dqt, ahead,
    pgrad, sib, gsum, y1, za1, za2, zb1, zb2, y2, dkv,
    send, recv, local,
):
    at = Place()
    net = Net(send, recv)
    c2 = HD ** (-0.5) * math.log2(math.e)
    loads = {}

    def load(name, src, dst):
        copy = pltpu.make_async_copy(src, dst, local.at[len(loads)])
        copy.start()
        loads[name] = copy

    def ready(*names):
        for name in names:
            loads[name].wait()

    for half in range(2):
        load("wq%d" % half, wq_h.at[pl.ds(half * 32, 32)], wq.at[half, at.z, at.y, at.c])
    load("byte", byte_h, byte)
    load("pq", pq_h, pool_q)
    load("pk", pk_h, pool_k)
    load("pv", pv_h, pool_v)
    load("po", po_h, pool_o)
    all_here = greet(partners(at))

    ready("byte", "pq", "pk", "pv")
    load("cot", cot_h, cots.at[at.t])
    load("wk", wk_h, wkv.at[:, pl.ds(0, HD)])
    load("wv", wv_h, wkv.at[:, pl.ds(HD, HD)])
    load("wo", wo_h, wo)
    pooled[...] = pool(lengths, byte, pool_q, pool_k, pool_v)
    ready("po")
    for i in range(8):
        cols = pl.ds(i * 512, 512)
        part[:, :, cols] = mm(pooled[...], pool_o[:, cols]).astype(BF16).reshape(NX, OWN, 512)
    ready("wq0", "wq1")
    all_here()

    def own(row, total):
        rows = total.astype(BF16)
        patches[pl.ds(row, 16), :] = rows
        hidden = rows.astype(F32)
        inv = lax.rsqrt(jnp.mean(hidden * hidden, -1, keepdims=True) + EPS)
        normed[at.t, pl.ds(row, 16), :] = (hidden * inv * gain[...].reshape(1, D).astype(F32)).astype(BF16)

    def patch_chain(k):
        yield from scatter_x(net, at, part, 16 * k, first.at[k], second.at[k], own)
        yield from gather_x(net, at, normed, 16 * k)

    chains = [patch_chain(0), patch_chain(1)]
    for chain in chains:
        next(chain)
    weights = gather_far(net, at, wq)
    next(weights)
    for turn in range(4):
        for chain in chains:
            next(chain, None)
        if turn < 3:
            next(weights)

    def normed_cols(i):
        return normed[:, :, columns(i)].reshape(ROWS, 512)

    ready("wk", "wv", "cot", "wo")
    acc[:, 0:2 * HD] = jnp.zeros((ROWS, 2 * HD), F32)

    @pl.loop(0, 8)
    def _(i):
        acc[:, 0:2 * HD] += mm(normed_cols(i), wkv[columns(i), :])

    for half in range(2):
        for which in range(2):
            block = acc[half * HALF:(half + 1) * HALF, which * HD:(which + 1) * HD]
            kvb[half, at.z, at.y, at.c, which] = block.astype(BF16)
    spread = gather(net, at, kvb)
    next(spread)
    cot_chains = [gather_x(net, at, cots, 0), gather_x(net, at, cots, 16)]
    for chain in cot_chains:
        next(chain)
    next(weights)
    next(spread)
    next(weights)
    next(spread)
    run([weights])
    acc[...] = jnp.zeros_like(acc)

    @pl.loop(0, 8)
    def _(i):
        w = jnp.concatenate([wq[half, i, y, c] for y in range(NY) for c in range(2) for half in range(2)], 0)
        acc[...] += mm(normed_cols(i), w)

    def prepare(block, straight, turned):
        straight[...] = stack(block.astype(BF16))
        turned[...] = straight[...].T

    prepare(acc[...] * c2, qs, qt)
    top[...] = jnp.full_like(top, NEG)
    mass[...] = jnp.zeros_like(mass)
    oacc[...] = jnp.zeros_like(oacc)
    column = lax.broadcasted_iota(jnp.int32, (KB, GROUP * ROWS), 1)
    key = lax.broadcasted_iota(jnp.int32, (KB, GROUP * ROWS), 0)
    ahead[...] = (key >> 6) * ROWS + (key & (HALF - 1)) - (column & (ROWS - 1))
    offsets = next(spread)

    def keys(half, z, which):
        return kvb[half, z, :, :, which].reshape(KB, HD)

    def scores(half, z, masked):
        out = mm(keys(half, z, 0), qt[...])
        if masked:
            base = lax.rem(at.s, 8) * ROWS - half * HALF
            out = jnp.where(ahead[...] <= base, out, NEG)
        return out

    def forward(z, masked):
        outs = [scores(half, z, masked) for half in range(2)]
        old = top[...]
        new = jnp.maximum(old, jnp.max(jnp.maximum(*outs), 0, keepdims=True))
        fade = jnp.exp2(old - new)
        ps = [jnp.exp2(out - new) for out in outs]
        mass[...] = mass[...] * fade + jnp.sum(ps[0] + ps[1], 0, keepdims=True)
        products = [dg(keys(half, z, 1), ps[half].astype(BF16), TN) for half in range(2)]
        oacc[...] = oacc[...] * fade + products[0] + products[1]
        top[...] = new

    def store_grads(half, z, grad_k, grad_v):
        pgrad[half, z, :, :, 0] = grad_k.astype(BF16).reshape(NY, 2, HALF, HD)
        pgrad[half, z, :, :, 1] = grad_v.astype(BF16).reshape(NY, 2, HALF, HD)

    def backward(z, masked):
        for half in range(2):
            prob = jnp.exp2(scores(half, z, masked) - lse[...])
            dprob = mm(keys(half, z, 1), gt[...])
            ds = (prob * (dprob - delta[...])).astype(BF16)
            store_grads(half, z, mm(ds, qs[...]) * math.log(2), mm(prob.astype(BF16), gs[...]))
            dqt[...] += dg(keys(half, z, 0), ds, TN)

    def tasks(body, z, otherwise=None):
        @pl.when(z < at.z)
        def _():
            body(z, False)

        @pl.when(z == at.z)
        def _():
            body(z, True)

        if otherwise is not None:

            @pl.when(z > at.z)
            def _():
                otherwise(z)

    def groups(body, offsets):
        if len(offsets) == 1:
            body(at.zz(offsets[0]))
        elif offsets:

            @pl.loop(0, 2)
            def _(k):
                body(at.zz(offsets[0] * (1 - 2 * k)))

    stage = 0
    while offsets is not None:
        groups(lambda z: tasks(forward, z), offsets)
        if stage == 0 or stage == 2:
            for chain in cot_chains:
                next(chain, None)
        if stage == 2:
            acc[...] = jnp.zeros_like(acc)

            @pl.loop(0, 8)
            def _(i):
                acc[...] += dg(cots[:, :, columns(i)].reshape(ROWS, 512), wo[:, columns(i)], NT)

            prepare(acc[...], gs, gt)
        stage += 1
        offsets = next(spread, None)

    ot = (oacc[...] / mass[...]).astype(BF16)
    lse[...] = top[...] + jnp.log2(mass[...])
    delta[...] = jnp.sum(gt[...].astype(F32) * ot.astype(F32), 0, keepdims=True)
    attn[...] = unstack(ot.T)
    dqt[...] = jnp.zeros_like(dqt)

    def nothing(z):
        zeros = jnp.zeros((KB, HD), F32)
        for half in range(2):
            store_grads(half, z, zeros, zeros)

    def out(half, total):
        dkv[half * HALF:(half + 1) * HALF, 0:HD] = total[0].astype(BF16)
        dkv[half * HALF:(half + 1) * HALF, HD:2 * HD] = total[1].astype(BF16)

    def layer_result(row, total):
        rows = pl.ds(row, 16)
        layer[rows, :] = (patches[rows, :].astype(F32) + total).astype(BF16)

    sums = scatter(net, at, pgrad, sib, gsum, y1, za1, za2, zb1, zb2, y2, out)
    for stage in range(5):
        groups(lambda z: tasks(backward, z, nothing), next(sums))
        if stage == 2:

            @pl.loop(0, 8)
            def _(i):
                cols = columns(i)
                part2[:, :, cols] = mm(attn[...], wo[:, cols]).astype(BF16).reshape(NX, OWN, 512)

            lay = [
                scatter_x(net, at, part2, 16 * k, first2.at[k], second2.at[k], layer_result)
                for k in range(2)
            ]
        if stage == 2 or stage == 4:
            for chain in lay:
                next(chain)
    next(sums)

    dq[...] = unstack((dqt[...] * HD ** (-0.5)).T.astype(BF16))
    next(sums)

    @pl.loop(0, 8)
    def _(i):
        w = jnp.concatenate([wq[half, i, y, c] for y in range(NY) for c in range(2) for half in range(2)], 0)
        grad_acc[:, columns(i)] = dg(dq[...], w, NT)

    run([sums])

    @pl.loop(0, 8)
    def _(i):
        rows = columns(i)
        total = grad_acc[:, rows] + dg(dkv[...], wkv[rows, :], NT)
        part3[:, :, rows] = total.astype(BF16).reshape(NX, OWN, 512)

    def grad_result(row, total):
        rows = pl.ds(row, 16)
        hidden = patches[rows, :].astype(F32)
        inv = lax.rsqrt(jnp.mean(hidden * hidden, -1, keepdims=True) + EPS)
        unit = hidden * inv
        scaled = total * gain[...].reshape(1, D).astype(F32)
        mean = jnp.mean(scaled * unit, -1, keepdims=True)
        cot = cots[at.t, rows, :].astype(F32)
        grad[rows, :] = (cot + inv * (scaled - unit * mean)).astype(BF16)

    run([scatter_x(net, at, part3, 16 * k, first3.at[k], second3.at[k], grad_result) for k in range(2)] + lay)
    net.finish()


def buf(*shape):
    return pltpu.VMEM(shape, BF16)


def wide(*shape):
    return pltpu.VMEM(shape, F32)


def finish_kernel(layer, grad, layer_out, patch_grad):
    layer_out[...] = layer[...]
    patch_grad[...] = grad[...]


def finish(layer, grad):
    here = pl.BlockSpec(memory_space=pltpu.VMEM)
    rows = jax.ShapeDtypeStruct((OWN, D), BF16)
    return tuple(
        pl.pallas_call(finish_kernel, out_shape=[rows, rows], in_specs=[here] * 2, out_specs=[here] * 2)(
            layer, grad
        )
    )


def on_device(
    byte_rows,
    patch_lengths,
    pool_query,
    pool_key,
    pool_value,
    pool_out,
    norm_gain,
    query_weight,
    key_weight,
    value_weight,
    out_weight,
    cotangent,
):
    heads = GROUP * HD
    here, there = pl.BlockSpec(memory_space=pltpu.VMEM), pl.BlockSpec(memory_space=pl.ANY)
    line = [buf(NX, OWN, D), buf(2, 2, 16, D // 2), buf(2, 2, 16, D)]
    half = (2, HALF, HD)
    scratch = [
        buf(*byte_rows.shape), buf(*pool_query.shape), buf(*pool_key.shape), buf(*pool_value.shape),
        buf(*pool_out.shape), buf(D, 2 * HD), buf(*out_weight.shape),
        buf(ROWS, 2 * HD), buf(OWN, D), buf(NX, OWN, D), buf(NX, OWN, D), buf(2, NZ, NY, 2, 32, heads),
        *line, *line, *line, wide(ROWS, D),
        wide(ROWS, heads), buf(ROWS, heads), buf(ROWS, heads),
        buf(2, NZ, NY, 2, *half), buf(heads, HD), buf(HD, heads), buf(heads, HD), buf(HD, heads),
        wide(1, heads), wide(1, heads), wide(HD, heads),
        wide(1, heads), wide(1, heads), wide(HD, heads), pltpu.VMEM((KB, heads), jnp.int32),
        buf(2, NZ, NY, 2, *half), buf(2, NZ, NY, *half), buf(2, NZ, NY, *half),
        buf(NZ, 3, *half), buf(*half), buf(3, 2, *half),
        buf(NY, *half), buf(3, 2, NY, *half), buf(3, *half),
        buf(ROWS, 2 * HD),
        pltpu.SemaphoreType.DMA((SENDS,)), pltpu.SemaphoreType.DMA((RECVS,)), pltpu.SemaphoreType.DMA((16,)),
    ]
    rows = jax.ShapeDtypeStruct((OWN, D), BF16)
    return finish(
        *pl.pallas_call(
            kernel,
            out_shape=[rows, rows],
            in_specs=[here] * 2 + [there] * 10,
            out_specs=[here] * 2,
            scratch_shapes=scratch,
            compiler_params=pltpu.CompilerParams(
                collective_id=1, has_side_effects=True, vmem_limit_bytes=VMEM
            ),
            cost_estimate=pl.CostEstimate(flops=10**10, bytes_accessed=1 << 24, transcendentals=0),
        )(
            patch_lengths, norm_gain, byte_rows, pool_query, pool_key, pool_value, pool_out,
            query_weight, key_weight, value_weight, out_weight, cotangent,
        )
    )


def solution(mesh):
    placed = (
        P("seq", None),
        P("seq", None),
        P(None, "tensor"),
        P(None, "tensor"),
        P(None, "tensor"),
        P("tensor", None),
        P(),
        P("seq", "tensor"),
        P(None, "tensor"),
        P(None, "tensor"),
        P("tensor", None),
        P(("seq", "tensor"), None),
    )
    return jax.shard_map(
        on_device,
        mesh=mesh,
        in_specs=placed,
        out_specs=(P(("seq", "tensor"), None), P(("seq", "tensor"), None)),
        check_vma=False,
    )
```

```python
import math

import jax
import jax.numpy as jnp
from jax import lax
from jax.experimental import pallas as pl
from jax.experimental.pallas import tpu as pltpu
from jax.sharding import PartitionSpec as P

EPS = 1e-05
NEG = -1e30
MESH = pl.DeviceIdType.MESH
NZ, NY, NX = 8, 4, 4
HD = 128
GROUP = 4
ROWS = 128
HALF = 64
SHARDS = 64
D = 4096
OWN = 32
KB = 512
SENDS, RECVS = 32, 128
VMEM = 56 * 1024 * 1024
F32 = jnp.float32
BF16 = jnp.bfloat16
NT = (((1,), (1,)), ((), ()))
TN = (((0,), (0,)), ((), ()))


def mm(a, b):
    return jnp.dot(a, b, preferred_element_type=F32)


def dg(a, b, dims):
    return lax.dot_general(a, b, dims, preferred_element_type=F32)


class Place:
    def __init__(self):
        s = lax.axis_index("seq")
        self.s = s
        self.z = lax.div(s, 8)
        self.y = lax.rem(lax.div(s, 2), 4)
        self.c = lax.rem(s, 2)
        self.t = lax.axis_index("tensor")
        self.sib = self.seq(self.z, self.y, 1 - self.c)
        self.up, self.down = self.along(1), self.along(-1)
        self.north = self.seq(self.z, self.yy(1), self.c)
        self.south = self.seq(self.z, self.yy(-1), self.c)
        self.across = self.seq(self.z, self.yy(2), self.c)

    def along(self, i):
        return self.seq(self.zz(i), self.y, self.c)

    def zz(self, i):
        return lax.rem(self.z + NZ + i, NZ)

    def yy(self, i):
        return lax.rem(self.y + NY + i, NY)

    def tt(self, i):
        return lax.rem(self.t + NX + i, NX)

    def seq(self, z, y, c):
        return (z * NY + y) * 2 + c


class Net:
    def __init__(self, send, recv):
        self.send, self.recv, self.all = send, recv, []

    def put(self, src, dst, **device):
        n = len(self.all)
        if n >= SENDS:
            self.all[n - SENDS].wait_send()
        copy = pltpu.make_async_remote_copy(
            src_ref=src,
            dst_ref=dst,
            send_sem=self.send.at[n % SENDS],
            recv_sem=self.recv.at[n % RECVS],
            device_id=device,
            device_id_type=MESH,
        )
        copy.start()
        self.all.append(copy)
        return copy

    def finish(self):
        for copy in self.all[-SENDS:]:
            copy.wait_send()


def greet(devices):
    barrier = pltpu.get_barrier_semaphore()
    for device in devices:
        pl.semaphore_signal(barrier, inc=1, device_id=device, device_id_type=MESH)
    return lambda: pl.semaphore_wait(barrier, len(devices))


def partners(at):
    ring = [{"seq": d} for d in (at.sib, at.up, at.down, at.north, at.south, at.across)]
    ring += [{"seq": at.along(i)} for i in (2, -2, 3, -3, 4)]
    return ring + [{"tensor": at.tt(1)}, {"tensor": at.tt(-1)}]


def run(chains):
    chains = list(chains)
    while chains:
        left = []
        for chain in chains:
            try:
                next(chain)
                left.append(chain)
            except StopIteration:
                pass
        chains = left


def same(net, view, **device):
    return net.put(view, view, **device)


def got(copies):
    for copy in copies:
        copy.wait_recv()


def gather(net, at, buf):
    n = buf.shape[4] // 2
    zz, yy, c, y, z = at.zz, at.yy, at.c, at.y, at.z
    both, every, low, high = pl.ds(0, 2), pl.ds(0, NY), pl.ds(0, n), pl.ds(n, n)

    def z_send(i):
        up, down = buf.at[0, zz(-i), y, c], buf.at[0, zz(i), y, c]
        if i == 3:
            up, down = up.at[low], down.at[high]
        return [same(net, up, seq=at.up), same(net, down, seq=at.down)]

    def y_send(half, *offsets):
        return [
            same(net, buf.at[half, zz(o), y, c], seq=to)
            for o in offsets
            for to in (at.across, at.north, at.south)
        ]

    def step(i, flows, units=range(4)):
        after = []
        for k, flow in zip(units, flows):
            got(flow)
            j, go = (0, -1, 1, 2)[k], []
            if i < 3 or k < 2:
                go.append(same(net, buf.at[1, zz(-i), yy(j), c], seq=at.up))
            if i < 3 or k >= 2:
                go.append(same(net, buf.at[1, zz(i), yy(j), c], seq=at.down))
            after.append(go)
        return after

    def share(*offsets):
        return [same(net, buf.at[both, zz(o), every, c], seq=at.sib) for o in offsets]

    across, north, south = y_send(1, 0)
    flows = step(0, [[]], (0,))
    zs = z_send(0)
    ys = [y_send(0, 0)]
    yield ()
    flows += step(0, [[north], [south], [across]], (1, 2, 3))
    got(zs)
    zs = z_send(1)
    ys.append(y_send(0, 1, -1))
    yield ()
    flows = step(1, flows)
    got(zs)
    zs = z_send(2)
    got(ys[0])
    sib = share(0)
    ys.append(y_send(0, 2, -2))
    yield ()
    flows = step(2, flows)
    got(zs)
    zs = z_send(3)
    got(ys[1])
    last, sib = sib, share(1, -1)
    ys.append(y_send(0, 3, -3))
    got(last)
    yield (0,)
    flows = step(3, flows)
    got(zs)
    ys.append(y_send(0, 4))
    got(ys[2])
    last, sib = sib, share(2, -2)
    got(last)
    yield (1, -1)
    got(sum(flows, []))
    got(ys[3])
    last, sib = sib, share(3, -3)
    got(last)
    yield (2, -2)
    got(ys[4])
    last, sib = sib, share(4)
    got(last)
    yield (3, -3)
    got(sib)
    yield (4,)


def gather_far(net, at, buf):
    zz, yy, c, y, z = at.zz, at.yy, at.c, at.y, at.z
    every, all_z = pl.ds(0, NY), pl.ds(0, NZ)
    y_ways = (at.across, at.north, at.south)

    def step(i, pairs):
        after = []
        for k in range(2):
            pair = pl.ds(2 * k, 2)
            got(pairs[k])
            go = []
            if i < 3 or k == 0:
                go.append(same(net, buf.at[1, zz(-i), pair, c], seq=at.up))
            if i < 3 or k == 1:
                go.append(same(net, buf.at[1, zz(i), pair, c], seq=at.down))
            after.append(go)
        return after

    def share(*offsets):
        return [same(net, buf.at[1, zz(o), every, c], seq=at.sib) for o in offsets]

    first = [same(net, buf.at[1, z, y, c], seq=to) for to in y_ways]
    zs = [same(net, buf.at[0, z, y, c], seq=at.along(i)) for i in (1, -1, 2, -2, 3, -3, 4)]
    yield
    got(first)
    pairs = step(0, [[], []])
    got(zs)
    ys = [same(net, buf.at[0, all_z, y, c], seq=to) for to in y_ways]
    sib = share(0)
    yield
    pairs = step(1, pairs)
    sib += share(1, -1)
    yield
    pairs = step(2, pairs)
    sib += share(2, -2)
    yield
    pairs = step(3, pairs)
    sib += share(3, -3)
    got(ys)
    sib += [same(net, buf.at[0, all_z, yy(j), c], seq=at.sib) for j in range(4)]
    yield
    got(pairs[0] + pairs[1])
    sib += share(4)
    yield
    got(sib)


def gather_x(net, at, buf, row):
    tt = at.tt
    rows, low, high = pl.ds(row, 16), pl.ds(0, D // 2), pl.ds(D // 2, D // 2)
    p = same(net, buf.at[at.t, rows], tensor=tt(1))
    m = same(net, buf.at[at.t, rows], tensor=tt(-1))
    yield
    p.wait_recv()
    m.wait_recv()
    p = same(net, buf.at[tt(-1), rows, low], tensor=tt(1))
    m = same(net, buf.at[tt(1), rows, high], tensor=tt(-1))
    yield
    p.wait_recv()
    m.wait_recv()


def add_into(ref, other):
    ref[...] = ref[...] + other[...]


def add_two(ref, one, two):
    ref[...] = (ref[...].astype(F32) + one[...].astype(F32) + two[...].astype(F32)).astype(BF16)


def scatter_x(net, at, part, row, first, second, result):
    tt = at.tt
    rows, low, high = pl.ds(row, 16), pl.ds(0, D // 2), pl.ds(D // 2, D // 2)
    p = net.put(part.at[tt(2), rows, low], first.at[0], tensor=tt(1))
    yield
    m = net.put(part.at[tt(2), rows, high], first.at[1], tensor=tt(-1))
    yield
    p.wait_recv()
    add_into(part.at[tt(1), rows, low], first.at[0])
    p = net.put(part.at[tt(1), rows], second.at[0], tensor=tt(1))
    m.wait_recv()
    add_into(part.at[tt(-1), rows, high], first.at[1])
    m = net.put(part.at[tt(-1), rows], second.at[1], tensor=tt(-1))
    yield
    p.wait_recv()
    m.wait_recv()
    mine = part[at.t, rows, :].astype(F32)
    result(row, mine + second[0].astype(F32) + second[1].astype(F32))


def slot(o):
    return o % NZ


def scatter(net, at, part, sib, acc, y_next, za_first, za_next, zb_first, zb_next, y_last, out):
    zz, yy = at.zz, at.yy
    both, every = pl.ds(0, 2), pl.ds(0, NY)
    one, two = pl.ds(0, 1), pl.ds(1, 1)
    low, high = pl.ds(0, 2), pl.ds(2, 2)
    ways = ((2, at.across), (1, at.north), (-1, at.south))
    near, ys, ring0, ring1 = {}, {}, {}, {}

    def share(offsets):
        for o in offsets:
            near[o] = net.put(part.at[both, zz(o), every, 1 - at.c], sib.at[both, zz(o)], seq=at.sib)

    def own(offsets):
        for o in offsets:
            near[o].wait_recv()
            z = zz(o)
            acc[:, z] = part[:, z, :, at.c] + sib[:, z]

    def y_send(offsets):
        for o in offsets:
            ys[o] = [
                net.put(acc.at[0, zz(o), yy(j)], y_next.at[slot(o), k], seq=to)
                for k, (j, to) in enumerate(ways)
            ]

    def y_sum(o, *came):
        got(ys[o])
        total = acc[0, zz(o), at.y].astype(F32)
        for k in range(3):
            total = total + y_next[slot(o), k].astype(F32)
        for ref in came:
            total = total + ref[...].astype(F32)
        return total

    def z_zero(i):
        if i < 4:
            got(ring0[i + 1])
        if i == 0:
            out(0, y_sum(0, za_next.at[0, 0], za_next.at[0, 1]))
            return
        for side, o in enumerate((i, -i)[:1 if i == 4 else 2]):
            came = [za_next.at[i, side]] if i < 3 else []
            acc[0, zz(o), at.y] = y_sum(o, *came).astype(BF16)
        if i == 3:
            add_into(acc.at[0, zz(3), at.y, one], za_first.at[one])
            add_into(acc.at[0, zz(-3), at.y, two], za_first.at[two])
        if i == 4:
            src = acc.at[0, zz(4), at.y]
            ring0[4] = [
                net.put(src.at[one], za_first.at[one], seq=at.up),
                net.put(src.at[two], za_first.at[two], seq=at.down),
            ]
            return
        ring0[i] = [
            net.put(acc.at[0, zz(i), at.y], za_next.at[i - 1, 0], seq=at.up),
            net.put(acc.at[0, zz(-i), at.y], za_next.at[i - 1, 1], seq=at.down),
        ]

    def z_one(i):
        if i == 4:
            ring1[4] = [
                net.put(acc.at[1, zz(4), low], zb_first.at[low], seq=at.up),
                net.put(acc.at[1, zz(4), high], zb_first.at[high], seq=at.down),
            ]
            return
        if i == 3:
            got(ring1[4])
            add_into(acc.at[1, zz(3), low], zb_first.at[low])
            add_into(acc.at[1, zz(-3), high], zb_first.at[high])
        go = []
        for k, pair in enumerate((low, high)):
            for side, o, to in ((0, i, at.up), (1, -i, at.down)):
                if i < 3:
                    ring1[i + 1][2 * k + side].wait_recv()
                    add_into(acc.at[1, zz(o), pair], zb_next.at[i, side, pair])
                go.append(net.put(acc.at[1, zz(o), pair], zb_next.at[i - 1, side, pair], seq=to))
        ring1[i] = go

    rounds = ((4,), (3, -3), (2, -2), (1, -1), (0,))
    yield rounds[0]
    share(rounds[0])
    for r in range(1, 5):
        yield rounds[r]
        share(rounds[r])
        own(rounds[r - 1])
        z_one(5 - r)
        y_send(rounds[r - 1])
        if r > 1:
            z_zero(6 - r)
    yield ()
    own(rounds[4])
    y_send(rounds[4])
    got(ring1[1])
    add_two(acc.at[1, at.z], zb_next.at[0, 0], zb_next.at[0, 1])
    last = [net.put(acc.at[1, at.z, yy(j)], y_last.at[k], seq=to) for k, (j, to) in enumerate(ways)]
    z_zero(1)
    yield ()
    got(last)
    block = acc[1, at.z, at.y].astype(F32)
    for k in range(3):
        block = block + y_last[k].astype(F32)
    out(1, block)
    z_zero(0)


def pool(lengths, byte, pool_query, pool_key, pool_value):
    nb = byte.shape[0]
    count = lengths[...].astype(F32)
    row = lax.broadcasted_iota(jnp.int32, (ROWS, ROWS), 0)
    col = lax.broadcasted_iota(jnp.int32, (ROWS, ROWS), 1)
    ends = jnp.sum(jnp.where(col <= row, count, 0.0), 1, keepdims=True)
    size = jnp.sum(jnp.where(col == row, count, 0.0), 1, keepdims=True)
    where_at = lax.broadcasted_iota(jnp.int32, (ROWS, nb), 1).astype(F32)
    member = (where_at >= ends - size) & (where_at < ends)
    sums = mm(jnp.where(member, 1.0, 0.0).astype(BF16), byte[...])
    means = (sums / size).astype(BF16)
    pq = mm(means, pool_query[...]).astype(BF16)
    pk = mm(byte[...], pool_key[...]).astype(BF16)
    pv = mm(byte[...], pool_value[...]).astype(BF16)
    heads = []
    for h in range(pq.shape[1] // HD):
        cols = slice(h * HD, (h + 1) * HD)
        scores = jnp.where(member, dg(pq[:, cols], pk[:, cols], NT) * HD ** (-0.5), NEG)
        expo = jnp.exp(scores - jnp.max(scores, -1, keepdims=True))
        weights = (expo / jnp.sum(expo, -1, keepdims=True)).astype(BF16)
        heads.append(mm(weights, pv[:, cols]))
    return jnp.concatenate(heads, 1).astype(BF16)


def stack(block):
    return jnp.concatenate([block[:, h * HD:(h + 1) * HD] for h in range(GROUP)], 0)


def unstack(value):
    return jnp.concatenate([value[h * ROWS:(h + 1) * ROWS] for h in range(GROUP)], 1)


def columns(i):
    return pl.ds(pl.multiple_of(i * 512, 512), 512)


def kernel(
    lengths, gain, byte_h, pq_h, pk_h, pv_h, po_h, wq_h, wk_h, wv_h, wo_h, cot_h,
    layer, grad,
    byte, pool_q, pool_k, pool_v, pool_o, wkv, wo, pooled, patches, normed, cots, wq,
    part, first, second, part2, first2, second2, part3, first3, second3, grad_acc,
    acc, attn, dq,
    kvb, qs, qt, gs, gt, top, mass, oacc, lse, delta, dqt, ahead,
    pgrad, sib, gsum, y1, za1, za2, zb1, zb2, y2, dkv,
    send, recv, local,
):
    at = Place()
    net = Net(send, recv)
    c2 = HD ** (-0.5) * math.log2(math.e)
    loads = {}

    def load(name, src, dst):
        copy = pltpu.make_async_copy(src, dst, local.at[len(loads)])
        copy.start()
        loads[name] = copy

    def ready(*names):
        for name in names:
            loads[name].wait()

    for half in range(2):
        load("wq%d" % half, wq_h.at[:, pl.ds(half * 256, 256)], wq.at[half, at.z, at.y, at.c])
    load("byte", byte_h, byte)
    load("pq", pq_h, pool_q)
    load("pk", pk_h, pool_k)
    load("pv", pv_h, pool_v)
    load("po", po_h, pool_o)
    all_here = greet(partners(at))

    ready("byte", "pq", "pk", "pv")
    load("cot", cot_h, cots.at[at.t])
    load("wk", wk_h, wkv.at[:, pl.ds(0, HD)])
    load("wv", wv_h, wkv.at[:, pl.ds(HD, HD)])
    load("wo", wo_h, wo)
    pooled[...] = pool(lengths, byte, pool_q, pool_k, pool_v)
    ready("po")
    for i in range(8):
        cols = pl.ds(i * 512, 512)
        part[:, :, cols] = mm(pooled[...], pool_o[:, cols]).astype(BF16).reshape(NX, OWN, 512)
    ready("wq0", "wq1")
    all_here()

    def own(row, total):
        rows = total.astype(BF16)
        patches[pl.ds(row, 16), :] = rows
        hidden = rows.astype(F32)
        inv = lax.rsqrt(jnp.mean(hidden * hidden, -1, keepdims=True) + EPS)
        normed[at.t, pl.ds(row, 16), :] = (hidden * inv * gain[...].reshape(1, D).astype(F32)).astype(BF16)

    def patch_chain(k):
        yield from scatter_x(net, at, part, 16 * k, first.at[k], second.at[k], own)
        yield from gather_x(net, at, normed, 16 * k)

    chains = [patch_chain(0), patch_chain(1)]
    for chain in chains:
        next(chain)
        next(chain)
    weights = gather_far(net, at, wq)
    next(weights)
    for turn in range(4):
        for chain in chains:
            next(chain, None)
        if turn < 3:
            next(weights)

    def normed_cols(i):
        return normed[:, :, columns(i)].reshape(ROWS, 512)

    ready("wk", "wv", "cot", "wo")
    acc[:, 0:2 * HD] = jnp.zeros((ROWS, 2 * HD), F32)

    @pl.loop(0, 8)
    def _(i):
        acc[:, 0:2 * HD] += mm(normed_cols(i), wkv[columns(i), :])

    for half in range(2):
        for which in range(2):
            block = acc[half * HALF:(half + 1) * HALF, which * HD:(which + 1) * HD]
            kvb[half, at.z, at.y, at.c, which] = block.astype(BF16)
    spread = gather(net, at, kvb)
    next(spread)
    cot_chains = [gather_x(net, at, cots, 0), gather_x(net, at, cots, 16)]
    for chain in cot_chains:
        next(chain)
    next(weights)
    next(spread)
    next(weights)
    next(spread)
    for chain in cot_chains:
        next(chain)
    run([weights])
    acc[...] = jnp.zeros_like(acc)

    @pl.loop(0, 8)
    def _(i):
        for half in range(2):
            acc[:, half * 256:(half + 1) * 256] += mm(normed_cols(i), wq[half, i].reshape(512, 256))

    def prepare(block, straight, turned):
        straight[...] = stack(block.astype(BF16))
        turned[...] = straight[...].T

    prepare(acc[...] * c2, qs, qt)
    top[...] = jnp.full_like(top, NEG)
    mass[...] = jnp.zeros_like(mass)
    oacc[...] = jnp.zeros_like(oacc)
    column = lax.broadcasted_iota(jnp.int32, (KB, GROUP * ROWS), 1)
    key = lax.broadcasted_iota(jnp.int32, (KB, GROUP * ROWS), 0)
    ahead[...] = (key >> 6) * ROWS + (key & (HALF - 1)) - (column & (ROWS - 1))
    offsets = next(spread)

    def keys(half, z, which):
        return kvb[half, z, :, :, which].reshape(KB, HD)

    def scores(half, z, masked):
        out = mm(keys(half, z, 0), qt[...])
        if masked:
            base = lax.rem(at.s, 8) * ROWS - half * HALF
            out = jnp.where(ahead[...] <= base, out, NEG)
        return out

    def forward(z, masked):
        outs = [scores(half, z, masked) for half in range(2)]
        old = top[...]
        new = jnp.maximum(old, jnp.max(jnp.maximum(*outs), 0, keepdims=True))
        fade = jnp.exp2(old - new)
        ps = [jnp.exp2(out - new) for out in outs]
        mass[...] = mass[...] * fade + jnp.sum(ps[0] + ps[1], 0, keepdims=True)
        products = [dg(keys(half, z, 1), ps[half].astype(BF16), TN) for half in range(2)]
        oacc[...] = oacc[...] * fade + products[0] + products[1]
        top[...] = new

    def store_grads(half, z, grad_k, grad_v):
        pgrad[half, z, :, :, 0] = grad_k.astype(BF16).reshape(NY, 2, HALF, HD)
        pgrad[half, z, :, :, 1] = grad_v.astype(BF16).reshape(NY, 2, HALF, HD)

    def backward(z, masked):
        for half in range(2):
            prob = jnp.exp2(scores(half, z, masked) - lse[...])
            dprob = mm(keys(half, z, 1), gt[...])
            ds = (prob * (dprob - delta[...])).astype(BF16)
            store_grads(half, z, mm(ds, qs[...]) * math.log(2), mm(prob.astype(BF16), gs[...]))
            dqt[...] += dg(keys(half, z, 0), ds, TN)

    def tasks(body, z, otherwise=None):
        @pl.when(z < at.z)
        def _():
            body(z, False)

        @pl.when(z == at.z)
        def _():
            body(z, True)

        if otherwise is not None:

            @pl.when(z > at.z)
            def _():
                otherwise(z)

    def groups(body, offsets):
        if len(offsets) == 1:
            body(at.zz(offsets[0]))
        elif offsets:

            @pl.loop(0, 2)
            def _(k):
                body(at.zz(offsets[0] * (1 - 2 * k)))

    stage = 0
    while offsets is not None:
        groups(lambda z: tasks(forward, z), offsets)
        if stage == 0:
            run(cot_chains)
            acc[...] = jnp.zeros_like(acc)

            @pl.loop(0, 8)
            def _(i):
                acc[...] += dg(cots[:, :, columns(i)].reshape(ROWS, 512), wo[:, columns(i)], NT)

            prepare(acc[...], gs, gt)
        stage += 1
        offsets = next(spread, None)

    ot = (oacc[...] / mass[...]).astype(BF16)
    lse[...] = top[...] + jnp.log2(mass[...])
    delta[...] = jnp.sum(gt[...].astype(F32) * ot.astype(F32), 0, keepdims=True)
    attn[...] = unstack(ot.T)
    dqt[...] = jnp.zeros_like(dqt)

    def nothing(z):
        zeros = jnp.zeros((KB, HD), F32)
        for half in range(2):
            store_grads(half, z, zeros, zeros)

    def out(half, total):
        dkv[half * HALF:(half + 1) * HALF, 0:HD] = total[0].astype(BF16)
        dkv[half * HALF:(half + 1) * HALF, HD:2 * HD] = total[1].astype(BF16)

    def layer_result(row, total):
        rows = pl.ds(row, 16)
        layer[rows, :] = (patches[rows, :].astype(F32) + total).astype(BF16)

    sums = scatter(net, at, pgrad, sib, gsum, y1, za1, za2, zb1, zb2, y2, out)
    for stage in range(5):
        groups(lambda z: tasks(backward, z, nothing), next(sums))
        if stage == 2:

            @pl.loop(0, 8)
            def _(i):
                cols = columns(i)
                part2[:, :, cols] = mm(attn[...], wo[:, cols]).astype(BF16).reshape(NX, OWN, 512)

            lay = [
                scatter_x(net, at, part2, 16 * k, first2.at[k], second2.at[k], layer_result)
                for k in range(2)
            ]
            for chain in lay:
                next(chain)
                next(chain)
        if stage == 4:
            for chain in lay:
                next(chain)
    next(sums)

    dq[...] = unstack((dqt[...] * HD ** (-0.5)).T.astype(BF16))

    def dq_product(i):
        grad_acc[:, columns(i)] = dg(dq[:, 0:256], wq[0, i].reshape(512, 256), NT) + dg(
            dq[:, 256:512], wq[1, i].reshape(512, 256), NT
        )

    pl.loop(0, 4)(dq_product)
    next(sums)
    pl.loop(4, 8)(dq_product)
    run([sums])

    def dkv_product(i):
        rows = columns(i)
        total = grad_acc[:, rows] + dg(dkv[...], wkv[rows, :], NT)
        part3[:, :, rows] = total.astype(BF16).reshape(NX, OWN, 512)

    def grad_result(row, total):
        rows = pl.ds(row, 16)
        hidden = patches[rows, :].astype(F32)
        inv = lax.rsqrt(jnp.mean(hidden * hidden, -1, keepdims=True) + EPS)
        unit = hidden * inv
        scaled = total * gain[...].reshape(1, D).astype(F32)
        mean = jnp.mean(scaled * unit, -1, keepdims=True)
        cot = cots[at.t, rows, :].astype(F32)
        grad[rows, :] = (cot + inv * (scaled - unit * mean)).astype(BF16)

    chains = [scatter_x(net, at, part3, 16 * k, first3.at[k], second3.at[k], grad_result) for k in range(2)]
    pl.loop(0, 4)(dkv_product)
    for chain in chains:
        next(chain)
    pl.loop(4, 8)(dkv_product)
    run(chains + lay)
    net.finish()


def buf(*shape):
    return pltpu.VMEM(shape, BF16)


def wide(*shape):
    return pltpu.VMEM(shape, F32)


def finish_kernel(layer, grad, layer_out, patch_grad):
    layer_out[...] = layer[...]
    patch_grad[...] = grad[...]


def finish(layer, grad):
    here = pl.BlockSpec(memory_space=pltpu.VMEM)
    rows = jax.ShapeDtypeStruct((OWN, D), BF16)
    return tuple(
        pl.pallas_call(finish_kernel, out_shape=[rows, rows], in_specs=[here] * 2, out_specs=[here] * 2)(
            layer, grad
        )
    )


def on_device(
    byte_rows,
    patch_lengths,
    pool_query,
    pool_key,
    pool_value,
    pool_out,
    norm_gain,
    query_weight,
    key_weight,
    value_weight,
    out_weight,
    cotangent,
):
    heads = GROUP * HD
    here, there = pl.BlockSpec(memory_space=pltpu.VMEM), pl.BlockSpec(memory_space=pl.ANY)
    line = [buf(NX, OWN, D), buf(2, 2, 16, D // 2), buf(2, 2, 16, D)]
    half = (2, HALF, HD)
    scratch = [
        buf(*byte_rows.shape), buf(*pool_query.shape), buf(*pool_key.shape), buf(*pool_value.shape),
        buf(*pool_out.shape), buf(D, 2 * HD), buf(*out_weight.shape),
        buf(ROWS, 2 * HD), buf(OWN, D), buf(NX, OWN, D), buf(NX, OWN, D), buf(2, NZ, NY, 2, 64, heads // 2),
        *line, *line, *line, wide(ROWS, D),
        wide(ROWS, heads), buf(ROWS, heads), buf(ROWS, heads),
        buf(2, NZ, NY, 2, *half), buf(heads, HD), buf(HD, heads), buf(heads, HD), buf(HD, heads),
        wide(1, heads), wide(1, heads), wide(HD, heads),
        wide(1, heads), wide(1, heads), wide(HD, heads), pltpu.VMEM((KB, heads), jnp.int32),
        buf(2, NZ, NY, 2, *half), buf(2, NZ, NY, *half), buf(2, NZ, NY, *half),
        buf(NZ, 3, *half), buf(*half), buf(3, 2, *half),
        buf(NY, *half), buf(3, 2, NY, *half), buf(3, *half),
        buf(ROWS, 2 * HD),
        pltpu.SemaphoreType.DMA((SENDS,)), pltpu.SemaphoreType.DMA((RECVS,)), pltpu.SemaphoreType.DMA((16,)),
    ]
    rows = jax.ShapeDtypeStruct((OWN, D), BF16)
    return finish(
        *pl.pallas_call(
            kernel,
            out_shape=[rows, rows],
            in_specs=[here] * 2 + [there] * 10,
            out_specs=[here] * 2,
            scratch_shapes=scratch,
            compiler_params=pltpu.CompilerParams(
                collective_id=1, has_side_effects=True, vmem_limit_bytes=VMEM
            ),
            cost_estimate=pl.CostEstimate(flops=10**10, bytes_accessed=1 << 24, transcendentals=0),
        )(
            patch_lengths, norm_gain, byte_rows, pool_query, pool_key, pool_value, pool_out,
            query_weight, key_weight, value_weight, out_weight, cotangent,
        )
    )


def solution(mesh):
    placed = (
        P("seq", None),
        P("seq", None),
        P(None, "tensor"),
        P(None, "tensor"),
        P(None, "tensor"),
        P("tensor", None),
        P(),
        P("seq", "tensor"),
        P(None, "tensor"),
        P(None, "tensor"),
        P("tensor", None),
        P(("seq", "tensor"), None),
    )
    return jax.shard_map(
        on_device,
        mesh=mesh,
        in_specs=placed,
        out_specs=(P(("seq", "tensor"), None), P(("seq", "tensor"), None)),
        check_vma=False,
    )
```
